32 devices in a mesh: fsdp: 16 (over z, y, x), tp: 2 (over core).
Axes of the slice: x: 2, y: 2, z: 4, core: 2. Of those that a mesh axis runs over, the one named last changes fastest.
Arguments:
- inputs: bfloat16 [2, 16, 256, 2048], P(None, 'fsdp', 'tp'), may hold values from -6 to 6
- cotangent: bfloat16 [2, 16, 256, 2048], P(None, 'fsdp', 'tp'), may hold values from -14 to 14
- joined_master: float32 [3, 2048, 2048], P(None, 'fsdp', 'tp'), may hold values from -0.125 to 0.125
- joined_first: float32 [3, 2048, 2048], P(None, 'fsdp', 'tp'), may hold values from -0.001953125 to 0.001953125
- joined_second: float32 [3, 2048, 2048], P(None, 'fsdp', 'tp'), may hold values from 1.9458863e-08 to 7.783545e-08
- outward_master: float32 [2048, 2048], P('fsdp', 'tp'), may hold values from -0.75 to 0.75
- outward_first: float32 [2048, 2048], P('fsdp', 'tp'), may hold values from -0.001953125 to 0.001953125
- outward_second: float32 [2048, 2048], P('fsdp', 'tp'), may hold values from 1.9458863e-08 to 7.783545e-08
- gated_master: float32 [2, 2048, 5632], P(None, 'fsdp', 'tp'), may hold values from -0.125 to 0.125
- gated_first: float32 [2, 2048, 5632], P(None, 'fsdp', 'tp'), may hold values from -0.001953125 to 0.001953125
- gated_second: float32 [2, 2048, 5632], P(None, 'fsdp', 'tp'), may hold values from 1.9458863e-08 to 7.783545e-08
- downward_master: float32 [2048, 5632], P('fsdp', 'tp'), may hold values from -2 to 2
- downward_first: float32 [2048, 5632], P('fsdp', 'tp'), may hold values from -0.001953125 to 0.001953125
- downward_second: float32 [2048, 5632], P('fsdp', 'tp'), may hold values from 1.9458863e-08 to 7.783545e-08
- vectors_master: float32 [5, 2048], P(None, 'fsdp'), may hold values from -1.5 to 3
- vectors_first: float32 [5, 2048], P(None, 'fsdp'), may hold values from -0.005859375 to 0.005859375
- vectors_second: float32 [5, 2048], P(None, 'fsdp'), may hold values from 1.7512977e-07 to 7.005191e-07
Outputs:
- outputs: bfloat16 [2, 16, 256, 2048], P(None, 'fsdp', 'tp')
- input_grad: bfloat16 [2, 16, 256, 2048], P(None, 'fsdp', 'tp')
- grad_norm: float32 [], replicated
- joined_updated: float32 [3, 2048, 2048], P(None, 'fsdp', 'tp')
- joined_moment: float32 [3, 2048, 2048], P(None, 'fsdp', 'tp')
- joined_variance: float32 [3, 2048, 2048], P(None, 'fsdp', 'tp')
- joined_copy: bfloat16 [3, 2048, 2048], P(None, 'fsdp', 'tp')
- outward_updated: float32 [2048, 2048], P('fsdp', 'tp')
- outward_moment: float32 [2048, 2048], P('fsdp', 'tp')
- outward_variance: float32 [2048, 2048], P('fsdp', 'tp')
- outward_copy: bfloat16 [2048, 2048], P('fsdp', 'tp')
- gated_updated: float32 [2, 2048, 5632], P(None, 'fsdp', 'tp')
- gated_moment: float32 [2, 2048, 5632], P(None, 'fsdp', 'tp')
- gated_variance: float32 [2, 2048, 5632], P(None, 'fsdp', 'tp')
- gated_copy: bfloat16 [2, 2048, 5632], P(None, 'fsdp', 'tp')
- downward_updated: float32 [2048, 5632], P('fsdp', 'tp')
- downward_moment: float32 [2048, 5632], P('fsdp', 'tp')
- downward_variance: float32 [2048, 5632], P('fsdp', 'tp')
- downward_copy: bfloat16 [2048, 5632], P('fsdp', 'tp')
- vectors_updated: float32 [5, 2048], P(None, 'fsdp')
- vectors_moment: float32 [5, 2048], P(None, 'fsdp')
- vectors_variance: float32 [5, 2048], P(None, 'fsdp')
- vectors_copy: bfloat16 [5, 2048], P(None, 'fsdp')
The draws below stay inside these ranges and needn't reach their ends.
All inputs are finite; a program needn't handle non-finite values.
Results may differ from the reference program's by a relative error of at most 0.012.
The reference program's roundings to bfloat16 on the way count: a program that leaves them out, or rounds other values in their place, can miss the bound.
Values may be sent and summed in bfloat16 or wider, within the bound.
No kernel may reach another device: no remote copies, remote signals or barrier semaphores. Data moves between devices by JAX's collectives and lax.ppermute only.
A program may use at most 256 MiB of HBM per device.

```python
import math
import jax
import jax.numpy as jnp
from jax import lax

D = 2048
H = 32
HD = 64
ROT = 16
FF = 5632
SEQ = 256
MICRO = 2
STEP = 5
SEQS = 16


def rising_scale(span_count, start_scale, rise_ratio):
    return start_scale * rise_ratio ** (jnp.arange(span_count, dtype=jnp.float32) / max(span_count - 1, 1))


def draw_cotangent(key, part):
    raw_values = jnp.clip(jax.random.normal(key, (MICRO, SEQS, SEQ, D), jnp.float32), -6.0, 6.0)
    column_scale = rising_scale(D, 0.6, 3.0)
    return (raw_values * column_scale).astype(jnp.bfloat16)


def draw_vectors_master(key, part):
    gain_key = jax.random.fold_in(key, 11)
    bias_key = jax.random.fold_in(key, 12)
    gains = rising_scale(D, 0.6, 3.0) * jax.random.uniform(gain_key, (D,), jnp.float32, 0.8, 1.25)
    biases = jnp.clip(0.3 * jax.random.normal(bias_key, (4, D), jnp.float32), -1.5, 1.5)
    return jnp.concatenate([gains[None, :], biases], axis=0)


def draw_downward_master(key, part):
    raw_values = jnp.clip(jax.random.normal(key, (D, FF), jnp.float32), -6.0, 6.0)
    column_scale = rising_scale(FF, 0.6, 3.0)
    return raw_values * FF ** (-0.5) * column_scale[None, :]


def block_levels(own_key, shape, split, low, high):
    level, own = 1.0, jax.random.fold_in(own_key, 6)
    for position, blocks in split:
        steps = jnp.exp(jax.random.uniform(jax.random.fold_in(own, position), (blocks,), jnp.float32, low / len(split), high / len(split)))
        level = level * jnp.repeat(steps, shape[position] // blocks).reshape([-1 if axis == position else 1 for axis in range(len(shape))])
    return level


def scatter_about(stream_key, shape, spread, bound, shards=(), held_as=jnp.bfloat16):
    array = jax.random.normal(stream_key, shape, jnp.float32) * spread
    if len(shards) > 0:
        array = block_levels(stream_key, shape, shards, -0.22, 0.18) * array
    return jnp.clip(array, min=-bound, max=bound).astype(held_as)


def setup_inputs(seed: int = 0) -> dict:
    seeds = jax.random.split(jax.random.key(seed), 18)
    inputs = scatter_about(seeds[0], (MICRO, SEQS, SEQ, D), 1.0, 6.0, ((1, 16), (2, 2)))
    cotangent = draw_cotangent(jax.random.fold_in(seeds[17], 71), 0)
    joined_master = scatter_about(seeds[2], (3, D, D), D ** -0.5, 0.125, ((1, 16), (2, 2)), jnp.float32)
    joined_first = scatter_about(seeds[3], (3, D, D), ((4 * D * D + 3 * D * FF + 5 * D) ** -0.5), 0.001953125, ((1, 16), (2, 2)), jnp.float32)
    joined_second = jnp.clip(jnp.exp(math.log(7.783545186157426e-08) - 1.3862944 * jax.random.uniform(seeds[4], (3, D, D), jnp.float32) ** block_levels(seeds[4], (3, D, D), ((1, 16), (2, 2)), -0.2, 0.2)), 1.9458862965393564e-08, 7.783545186157426e-08)
    outward_master = scatter_about(seeds[5], (D, D), (D // 32) ** -0.5, 0.75, ((0, 16), (1, 2)), jnp.float32)
    outward_first = scatter_about(seeds[6], (D, D), ((4 * D * D + 3 * D * FF + 5 * D) ** -0.5), 0.001953125, ((0, 16), (1, 2)), jnp.float32)
    outward_second = jnp.clip(jnp.exp(math.log(7.783545186157426e-08) - 1.3862944 * jax.random.uniform(seeds[7], (D, D), jnp.float32) ** block_levels(seeds[7], (D, D), ((0, 16), (1, 2)), -0.2, 0.2)), 1.9458862965393564e-08, 7.783545186157426e-08)
    gated_master = scatter_about(seeds[8], (2, D, FF), D ** -0.5, 0.125, ((1, 16), (2, 2)), jnp.float32)
    gated_first = scatter_about(seeds[9], (2, D, FF), ((4 * D * D + 3 * D * FF + 5 * D) ** -0.5), 0.001953125, ((1, 16), (2, 2)), jnp.float32)
    gated_second = jnp.clip(jnp.exp(math.log(7.783545186157426e-08) - 1.3862944 * jax.random.uniform(seeds[10], (2, D, FF), jnp.float32) ** block_levels(seeds[10], (2, D, FF), ((1, 16), (2, 2)), -0.2, 0.2)), 1.9458862965393564e-08, 7.783545186157426e-08)
    downward_master = draw_downward_master(jax.random.fold_in(seeds[17], 71), 0)
    downward_first = scatter_about(seeds[12], (D, FF), ((4 * D * D + 3 * D * FF + 5 * D) ** -0.5), 0.001953125, ((0, 16), (1, 2)), jnp.float32)
    downward_second = jnp.clip(jnp.exp(math.log(7.783545186157426e-08) - 1.3862944 * jax.random.uniform(seeds[13], (D, FF), jnp.float32) ** block_levels(seeds[13], (D, FF), ((0, 16), (1, 2)), -0.2, 0.2)), 1.9458862965393564e-08, 7.783545186157426e-08)
    vectors_master = draw_vectors_master(jax.random.fold_in(seeds[17], 71), 0)
    vectors_first = scatter_about(seeds[15], (5, D), (3 * (4 * D * D + 3 * D * FF + 5 * D) ** -0.5), 0.005859375, ((1, 16),), jnp.float32)
    vectors_second = jnp.clip(jnp.exp(math.log(7.00519080965023e-07) - 1.3862944 * jax.random.uniform(seeds[16], (5, D), jnp.float32) ** block_levels(seeds[16], (5, D), ((1, 16),), -0.2, 0.2)), 1.7512977024125576e-07, 7.00519080965023e-07)
    return dict(inputs=inputs, cotangent=cotangent, joined_master=joined_master, joined_first=joined_first, joined_second=joined_second, outward_master=outward_master, outward_first=outward_first, outward_second=outward_second, gated_master=gated_master, gated_first=gated_first, gated_second=gated_second, downward_master=downward_master, downward_first=downward_first, downward_second=downward_second, vectors_master=vectors_master, vectors_first=vectors_first, vectors_second=vectors_second)


@jax.custom_vjp
def low(v):
    return lax.optimization_barrier(v.astype(jnp.bfloat16)).astype(jnp.float32)

@jax.custom_vjp
def low_back(v):
    return v

def low_keep(v):
    return (low(v), None)

def low_pass(kept, grad):
    return (grad,)

def back_keep(v):
    return (v, None)

def back_low(kept, grad):
    return (low(grad),)
low.defvjp(low_keep, low_pass)
low_back.defvjp(back_keep, back_low)
EPS_NORM = 1e-05
CLIP = 1.0
BETA_ONE = 0.5
BETA_TWO = 0.5
ADAM_EPS = 1e-08
DECAY = 0.1
SMALL_RATE = 0.2
ROPE_BASE = 10000.0
HIGHEST = lax.Precision.HIGHEST

def normalize(row_block, row_gain, row_shift):
    average = lax.optimization_barrier(jnp.mean(row_block, axis=-1, keepdims=True))
    centred = row_block - average
    variance = lax.optimization_barrier(jnp.mean(centred * centred, axis=-1, keepdims=True))
    return centred * lax.rsqrt(variance + EPS_NORM) * row_gain + row_shift

def rotary(head_rows, length, rot_dims):
    half_dims = rot_dims // 2
    frequency = ROPE_BASE ** (-(2.0 * jnp.arange(half_dims, dtype=jnp.float32)) / rot_dims)
    angles = jnp.arange(length, dtype=jnp.float32)[:, None] * frequency[None, :]
    cosine_table = jnp.concatenate([jnp.cos(angles), jnp.cos(angles)], axis=-1)[:, None, :]
    sine_table = jnp.concatenate([jnp.sin(angles), jnp.sin(angles)], axis=-1)[:, None, :]
    rotated_part = head_rows[..., :rot_dims]
    first_half = rotated_part[..., :half_dims]
    second_half = rotated_part[..., half_dims:]
    turned = jnp.concatenate([-second_half, first_half], axis=-1)
    return jnp.concatenate([rotated_part * cosine_table + turned * sine_table, head_rows[..., rot_dims:]], axis=-1)

def layer(params, row_block):
    joined_weight, outward_weight, gated_weight, downward_weight, vector_rows = params
    length = row_block.shape[0]
    normed = low(normalize(row_block, vector_rows[0], vector_rows[1]))
    joined_out = jnp.einsum('td,cde->cte', normed, joined_weight, precision=HIGHEST) + vector_rows[2:5][:, None, :]
    joined_out = low_back(joined_out)
    heads_all = joined_out.reshape(3, length, H, HD)
    query = low(rotary(heads_all[0], length, ROT))
    keys = low(rotary(heads_all[1], length, ROT))
    values = low(heads_all[2])
    scores = low_back(jnp.einsum('thd,shd->hts', query, keys, precision=HIGHEST) * HD ** (-0.5))
    causal = jnp.arange(length)[:, None] >= jnp.arange(length)[None, :]
    scores = jnp.where(causal[None], scores, -jnp.inf)
    probs = low(jax.nn.softmax(scores, axis=-1))
    mixed = jnp.einsum('hts,shd->thd', probs, values, precision=HIGHEST).reshape(length, D)
    mixed = low(low_back(mixed))
    attn_part = jnp.dot(mixed, outward_weight.T, precision=HIGHEST)
    gate_up = low_back(jnp.einsum('td,cdf->ctf', normed, gated_weight, precision=HIGHEST))
    activated = low(jax.nn.silu(gate_up[0]) * gate_up[1])
    mlp_part = jnp.dot(activated, downward_weight.T, precision=HIGHEST)
    return row_block + attn_part + mlp_part

def adamw(master, first_old, second_old, gradient, factor, step_rate, weight_decay):
    clipped = gradient * factor
    moment = BETA_ONE * first_old + (1.0 - BETA_ONE) * clipped
    variance = BETA_TWO * second_old + (1.0 - BETA_TWO) * clipped * clipped
    moment_hat = moment / (1.0 - BETA_ONE ** STEP)
    variance_hat = variance / (1.0 - BETA_TWO ** STEP)
    updated = master - step_rate * (moment_hat / (jnp.sqrt(variance_hat) + ADAM_EPS) + weight_decay * master)
    return (updated, moment, variance, updated.astype(jnp.bfloat16))

def reference(inputs, cotangent, joined_master, joined_first, joined_second, outward_master, outward_first, outward_second, gated_master, gated_first, gated_second, downward_master, downward_first, downward_second, vectors_master, vectors_first, vectors_second):
    masters = (joined_master, outward_master, gated_master, downward_master, vectors_master)
    params = tuple((low(weight_piece) for weight_piece in masters))
    seq_count = MICRO * SEQS
    group_size = math.gcd(seq_count, max(1, 4096 // SEQ))
    row_groups = inputs.astype(jnp.float32).reshape(seq_count // group_size, group_size, SEQ, D)
    back_groups = cotangent.astype(jnp.float32).reshape(seq_count // group_size, group_size, SEQ, D)

    def run_group(weights, batch):
        return jax.vmap(lambda one_seq: layer(weights, one_seq))(batch)

    def one_group(totals, pair):
        row_group, back_group = pair
        results, pull = jax.vjp(run_group, params, row_group)
        param_grads, row_grads = pull(back_group)
        totals = tuple((acc + new_term for acc, new_term in zip(totals, param_grads)))
        return (totals, (results.astype(jnp.bfloat16), row_grads.astype(jnp.bfloat16)))
    zeros_init = tuple((jnp.zeros(weight_piece.shape, jnp.float32) for weight_piece in masters))
    gradients, (results, row_grads) = lax.scan(one_group, zeros_init, (row_groups, back_groups))
    outputs = results.reshape(MICRO, SEQS, SEQ, D)
    input_grad = row_grads.reshape(MICRO, SEQS, SEQ, D)
    square_total = jnp.float32(0.0)
    for grad_piece in gradients:
        square_total = square_total + jnp.sum(grad_piece * grad_piece)
    grad_norm = jnp.sqrt(square_total)
    factor = jnp.minimum(1.0, CLIP / (grad_norm + 1e-06))
    joined_new = adamw(joined_master, joined_first, joined_second, gradients[0], factor, D ** (-0.5), DECAY)
    outward_new = adamw(outward_master, outward_first, outward_second, gradients[1], factor, (D // 32) ** (-0.5), DECAY)
    gated_new = adamw(gated_master, gated_first, gated_second, gradients[2], factor, D ** (-0.5), DECAY)
    downward_new = adamw(downward_master, downward_first, downward_second, gradients[3], factor, FF ** (-0.5), DECAY)
    vectors_new = adamw(vectors_master, vectors_first, vectors_second, gradients[4], factor, SMALL_RATE, 0.0)
    return (outputs, input_grad, grad_norm, joined_new[0], joined_new[1], joined_new[2], joined_new[3], outward_new[0], outward_new[1], outward_new[2], outward_new[3], gated_new[0], gated_new[1], gated_new[2], gated_new[3], downward_new[0], downward_new[1], downward_new[2], downward_new[3], vectors_new[0], vectors_new[1], vectors_new[2], vectors_new[3])
```

```python
import functools
import jax
import jax.numpy as jnp
from jax import lax
from jax.experimental import pallas as pl
from jax.experimental.pallas import tpu as pltpu
from jax.sharding import Mesh
from jax.sharding import PartitionSpec as P

HD = 64
ROT = 16
MICRO = 2
STEP = 5
QUAD = 4

EPS_NORM = 1e-05
CLIP = 1.0
BETA_ONE = 0.5
BETA_TWO = 0.5
ADAM_EPS = 1e-08
DECAY = 0.1
SMALL_RATE = 0.2
ROPE_BASE = 10000.0
LOW = jnp.bfloat16
F32 = jnp.float32
SWAP = [(0, 1), (1, 0)]


def nn(left, right):
    return lax.dot_general(left, right, (((1,), (0,)), ((), ())), preferred_element_type=F32)


def nt(left, right):
    return lax.dot_general(left, right, (((1,), (1,)), ((), ())), preferred_element_type=F32)


def tn(left, right):
    return lax.dot_general(left, right, (((0,), (0,)), ((), ())), preferred_element_type=F32)


def swap(value, axis):
    return lax.ppermute(value, axis, SWAP)


def gate_kernel(*refs):
    pass


def after(value, *others):
    anywhere = pl.BlockSpec(memory_space=pl.ANY)
    return pl.pallas_call(
        gate_kernel,
        in_specs=[anywhere] * (1 + len(others)),
        out_specs=anywhere,
        out_shape=jax.ShapeDtypeStruct(value.shape, value.dtype),
        input_output_aliases={0: 0},
        name="after",
    )(value, *others)


def gather_line(block, place):
    ups, downs = [block], [block]
    for step in range(1, QUAD):
        ups.append(lax.ppermute(ups[-1], "a", [(i, i + 1) for i in range(step - 1, QUAD - 1)]))
        downs.append(lax.ppermute(downs[-1], "a", [(i, i - 1) for i in range(1, QUAD - step + 1)]))
    whole = jnp.zeros((QUAD,) + block.shape, block.dtype)
    whole = lax.dynamic_update_index_in_dim(whole, block, 0, 0)
    for k in range(1, QUAD):
        picked = jnp.where(place + k < QUAD, downs[k], ups[QUAD - k])
        whole = lax.dynamic_update_index_in_dim(whole, picked, k, 0)
    return whole, downs[-1]


def add_low(left, right):
    return (left.astype(F32) + right.astype(F32)).astype(LOW)


def scatter_line(parts):
    up = down = None
    for step in range(1, QUAD):
        to_up, to_down = parts[QUAD - step], parts[step]
        if step > 1:
            to_up, to_down = add_low(to_up, up), add_low(to_down, down)
        up = lax.ppermute(to_up, "a", [(i, i + 1) for i in range(0, step)])
        down = lax.ppermute(to_down, "a", [(i, i - 1) for i in range(QUAD - step, QUAD)])
    return parts[0].astype(F32) + up.astype(F32) + down.astype(F32)


def bits(axis):
    found, bit = [], 1
    count, at = lax.axis_size(axis), lax.axis_index(axis)
    while bit < count:
        found.append((axis, [(i, i ^ bit) for i in range(count)], (at // bit) % 2))
        bit *= 2
    return found


def gather_small(value):
    for axis, pairs, bit in bits("p") + bits("a"):
        other = lax.ppermute(value, axis, pairs)
        value = jnp.where(
            bit == 0,
            jnp.concatenate([value, other], axis=-1),
            jnp.concatenate([other, value], axis=-1),
        )
    return value


def sum_small(value):
    for axis, pairs, bit in bits("tp") + bits("p") + bits("a"):
        value = value + lax.ppermute(value, axis, pairs)
    return value


def attention_kernel(
    mask_ref, cos_ref, left_ref, right_ref, bias_ref, joined_ref, back_ref, mixed_ref, grad_ref, bias_grad_ref
):
    rows, width = cos_ref.shape
    heads = width // HD
    scale = HD ** (-0.5)
    joined = joined_ref[...].reshape(rows, 3 * width) + bias_ref[0:1, :]
    cos, left, right = cos_ref[...], left_ref[...], right_ref[...]

    def turn(v):
        return v * cos + pltpu.roll(v, width - ROT // 2, 1) * left + pltpu.roll(v, ROT // 2, 1) * right

    def turn_back(g):
        return g * cos - (pltpu.roll(g, width - ROT // 2, 1) * left + pltpu.roll(g, ROT // 2, 1) * right)

    query = turn(joined[:, :width]).astype(LOW)
    keys = turn(joined[:, width : 2 * width]).astype(LOW)
    values = joined[:, 2 * width :].astype(LOW)
    back = back_ref[...].reshape(rows, width)
    mask = mask_ref[...]
    mixed, d_query, d_keys, d_values = [], [], [], []
    for head in range(heads):
        cut = slice(head * HD, (head + 1) * HD)
        q, k, v, g = query[:, cut], keys[:, cut], values[:, cut], back[:, cut]
        scores = nt(q, k) * scale + mask
        peak = jnp.max(scores, axis=-1, keepdims=True)
        raised = jnp.exp(scores - peak)
        full = raised / jnp.sum(raised, axis=-1, keepdims=True)
        probs = full.astype(LOW)
        mixed.append(nn(probs, v))
        prob_grad = nt(g, v)
        weighted = full * prob_grad
        inner = jnp.sum(weighted, axis=-1, keepdims=True)
        score_grad = (weighted - full * inner).astype(LOW)
        d_query.append(nn(score_grad, k) * scale)
        d_keys.append(tn(score_grad, q) * scale)
        d_values.append(tn(probs, g))
    mixed_ref[...] = jnp.concatenate(mixed, axis=-1).astype(LOW).reshape(mixed_ref.shape)
    out = jnp.concatenate(
        [
            turn_back(jnp.concatenate(d_query, axis=-1)),
            turn_back(jnp.concatenate(d_keys, axis=-1)),
            jnp.concatenate(d_values, axis=-1),
        ],
        axis=-1,
    ).astype(LOW)
    grad_ref[...] = out.reshape(grad_ref.shape)

    @pl.when(pl.program_id(0) == 0)
    def _():
        bias_grad_ref[...] = jnp.zeros_like(bias_grad_ref)

    sums = jnp.sum(out.astype(F32).reshape(rows // 8, 8, 3 * width), axis=0)
    bias_grad_ref[...] += sums


def attention(joined, back, bias, tp_index):
    tokens, width = back.shape
    half = 128
    seqs = tokens // (2 * half)
    length = 2 * half
    position = lax.rem(jnp.arange(length) + tp_index * half, length)
    mask = jnp.where(position[:, None] >= position[None, :], 0.0, -jnp.inf).astype(F32)
    frequency = ROPE_BASE ** (-(2.0 * jnp.arange(ROT // 2, dtype=F32)) / ROT)
    angles = position.astype(F32)[:, None] * frequency[None, :]
    cosine, sine = jnp.cos(angles), jnp.sin(angles)
    rest = jnp.ones((length, HD - ROT), F32)
    nothing = jnp.zeros((length, ROT // 2), F32)
    heads = width // HD
    cos = jnp.tile(jnp.concatenate([cosine, cosine, rest], 1), (1, heads))
    left = jnp.tile(jnp.concatenate([-sine, nothing, 0.0 * rest], 1), (1, heads))
    right = jnp.tile(jnp.concatenate([nothing, sine, 0.0 * rest], 1), (1, heads))
    fixed = lambda i: (0, 0)
    rows = lambda i: (0, i, 0, 0)
    shape = lambda w: (2, seqs, half, w)
    mixed, grad, bias_grad = pl.pallas_call(
        attention_kernel,
        grid=(seqs,),
        in_specs=[
            pl.BlockSpec((length, length), fixed),
            pl.BlockSpec((length, width), fixed),
            pl.BlockSpec((length, width), fixed),
            pl.BlockSpec((length, width), fixed),
            pl.BlockSpec((1, 3 * width), fixed),
            pl.BlockSpec((2, 1, half, 3 * width), rows),
            pl.BlockSpec((2, 1, half, width), rows),
        ],
        out_specs=[
            pl.BlockSpec((2, 1, half, width), rows),
            pl.BlockSpec((2, 1, half, 3 * width), rows),
            pl.BlockSpec((8, 3 * width), fixed),
        ],
        out_shape=[
            jax.ShapeDtypeStruct(shape(width), LOW),
            jax.ShapeDtypeStruct(shape(3 * width), LOW),
            jax.ShapeDtypeStruct((8, 3 * width), F32),
        ],
        cost_estimate=pl.CostEstimate(
            flops=seqs * heads * 7 * 2 * length * length * HD * 4,
            bytes_accessed=tokens * width * 30,
            transcendentals=seqs * heads * length * length,
        ),
        compiler_params=pltpu.CompilerParams(vmem_limit_bytes=32 * 1024 * 1024),
        name="attention_both_ways",
    )(mask, cos, left, right, bias, joined.reshape(shape(3 * width)), back.reshape(shape(width)))
    return (
        mixed.reshape(tokens, width),
        grad.reshape(tokens, 3 * width),
        jnp.sum(bias_grad, axis=0),
    )


def product_kernel(terms, *refs):
    out_ref = refs[2 * terms]
    total = nt(refs[0][...], refs[terms][...])
    for term in range(1, terms):
        total += nt(refs[term][...], refs[terms + term][...])
    out_ref[...] = total.astype(out_ref.dtype)


def product_grad_kernel(terms, *refs):
    xhat_ref, out_ref, sums_ref = refs[2 * terms :]
    total = nt(refs[0][...], refs[terms][...])
    for term in range(1, terms):
        total += nt(refs[term][...], refs[terms + term][...])
    out_ref[...] = total.astype(out_ref.dtype)
    xhat = xhat_ref[...].astype(F32)

    @pl.when(pl.program_id(1) == 0)
    def _():
        sums_ref[...] = jnp.zeros_like(sums_ref)

    tall = total.shape[0] // 8
    sums_ref[0:8, :] += jnp.sum((total * xhat).reshape(tall, 8, -1), axis=0)
    sums_ref[8:16, :] += jnp.sum(total.reshape(tall, 8, -1), axis=0)


def product_sum(pairs, tokens, depth, extra=None):
    tall, broad = 512, 512
    terms = len(pairs)
    lefts = [pl.BlockSpec((tall, left.shape[1]), lambda j, i: (i, 0)) for left, _, _ in pairs]
    rights = [
        pl.BlockSpec((broad, left.shape[1]), functools.partial(lambda at, j, i: (j, at), at))
        for left, _, at in pairs
    ]
    deep = sum(left.shape[1] for left, _, _ in pairs)
    in_specs, operands = lefts + rights, [p[0] for p in pairs] + [p[1] for p in pairs]
    out_specs = pl.BlockSpec((tall, broad), lambda j, i: (i, j))
    out_shape = jax.ShapeDtypeStruct((tokens, depth), LOW)
    kernel = product_kernel
    if extra is not None:
        kernel = product_grad_kernel
        in_specs = in_specs + [
            pl.BlockSpec((tall, broad), lambda j, i: (i, j)),
        ]
        operands = operands + list(extra)
        out_specs = [out_specs, pl.BlockSpec((16, broad), lambda j, i: (0, j))]
        out_shape = [out_shape, jax.ShapeDtypeStruct((16, depth), F32)]
    return pl.pallas_call(
        functools.partial(kernel, terms),
        grid=(depth // broad, tokens // tall),
        in_specs=in_specs,
        out_specs=out_specs,
        out_shape=out_shape,
        cost_estimate=pl.CostEstimate(
            flops=2 * tokens * depth * deep,
            bytes_accessed=2 * (depth + tokens) * deep + 2 * tokens * depth,
            transcendentals=0,
        ),
        compiler_params=pltpu.CompilerParams(vmem_limit_bytes=48 * 1024 * 1024),
        name="product_sum",
    )(*operands)


def norm_kernel(gain_ref, shift_ref, own_ref, other_ref, normed_ref, xhat_ref):
    def run(ref):
        rows = ref[...].astype(F32)
        average = jnp.mean(rows, axis=-1, keepdims=True)
        centred = rows - average
        variance = jnp.mean(centred * centred, axis=-1, keepdims=True)
        xhat = centred * lax.rsqrt(variance + EPS_NORM)
        xhat_ref[...] = xhat.astype(LOW)
        normed_ref[...] = (xhat * gain_ref[...] + shift_ref[...]).astype(LOW)

    half = pl.num_programs(0) // 2

    @pl.when(pl.program_id(0) < half)
    def _():
        run(own_ref)

    @pl.when(pl.program_id(0) >= half)
    def _():
        run(other_ref)


def norm_rows(own, other, gain, shift):
    rows, depth = own.shape
    tall = 256
    half = rows // tall
    fixed = lambda i: (0, 0)
    return pl.pallas_call(
        norm_kernel,
        grid=(2 * half,),
        in_specs=[
            pl.BlockSpec((1, depth), fixed),
            pl.BlockSpec((1, depth), fixed),
            pl.BlockSpec((tall, depth), lambda i: (jnp.minimum(i, half - 1), 0)),
            pl.BlockSpec((tall, depth), lambda i: (jnp.maximum(i - half, 0), 0)),
        ],
        out_specs=[pl.BlockSpec((tall, depth), lambda i: (i, 0))] * 2,
        out_shape=[jax.ShapeDtypeStruct((2 * rows, depth), LOW)] * 2,
        cost_estimate=pl.CostEstimate(
            flops=20 * rows * depth, bytes_accessed=12 * rows * depth, transcendentals=0
        ),
        compiler_params=pltpu.CompilerParams(vmem_limit_bytes=32 * 1024 * 1024),
        name="norm_rows",
    )(gain, shift, own, other)


def adamw(master, first_old, second_old, gradient, factor, step_rate, weight_decay):
    clipped = gradient * factor
    moment = BETA_ONE * first_old + (1.0 - BETA_ONE) * clipped
    variance = BETA_TWO * second_old + (1.0 - BETA_TWO) * clipped * clipped
    moment_hat = moment / (1.0 - BETA_ONE**STEP)
    variance_hat = variance / (1.0 - BETA_TWO**STEP)
    updated = master - step_rate * (
        moment_hat / (jnp.sqrt(variance_hat) + ADAM_EPS) + weight_decay * master
    )
    return (updated, moment, variance, updated.astype(LOW))


def on_device(
    inputs,
    cotangent,
    joined_master,
    joined_first,
    joined_second,
    outward_master,
    outward_first,
    outward_second,
    gated_master,
    gated_first,
    gated_second,
    downward_master,
    downward_first,
    downward_second,
    vectors_master,
    vectors_first,
    vectors_second,
):
    tp_count = lax.axis_size("tp")
    quads = lax.axis_size("p")
    place = lax.axis_index("a")
    at_p = lax.axis_index("p")
    tp_index = lax.axis_index("tp")
    depth = inputs.shape[-1]
    rows_here = joined_master.shape[1]
    att_width = joined_master.shape[2] // QUAD
    ff_here = gated_master.shape[2]
    tiles = ff_here // 128
    wide = -(-tiles // QUAD)
    ff_width = wide * 128
    shortage = wide * QUAD - tiles
    parts = 2
    ff_part = ff_width // parts

    starts, lengths = [], []
    for index in range(QUAD):
        lacks = max(0, index - (QUAD - shortage))
        starts.append((index * wide - lacks) * 128)
        lengths.append((wide - (1 if index >= QUAD - shortage else 0)) * 128)

    def reorder(value):
        shape = value.shape[:-1]
        split = value.reshape(shape + (QUAD, quads, rows_here))
        return jnp.swapaxes(split, -3, -2).reshape(shape + (depth,))

    def restore(value):
        shape = value.shape[:-1]
        split = value.reshape(shape + (quads, QUAD, rows_here))
        return jnp.swapaxes(split, -3, -2).reshape(shape + (depth,))

    def attention_piece(index):
        cut = slice(index * att_width, (index + 1) * att_width)
        return jnp.concatenate(
            [joined_master[c][:, cut] for c in range(3)] + [outward_master[:, cut]], axis=1
        ).astype(LOW)

    def hidden_piece(part, index):
        low, high = part * ff_part, min((part + 1) * ff_part, lengths[index])
        first, last = starts[index] + low, starts[index] + high

        def cut(w):
            return jnp.pad(w[:, first:last], ((0, 0), (0, ff_part - (last - first))))

        return jnp.concatenate(
            [cut(gated_master[0]), cut(gated_master[1]), cut(downward_master)], axis=1
        ).astype(LOW)

    def gather_weight(make):
        pieces = jnp.stack([make(index) for index in range(QUAD)])
        mine = lax.all_to_all(pieces, "a", 0, 0, tiled=True)
        return lax.all_gather(mine, "p", axis=0).reshape(depth, pieces.shape[-1])

    attention_weight = gather_weight(attention_piece)

    vectors_full = gather_small(vectors_master.astype(LOW)).astype(F32)
    row_gain, row_shift = reorder(vectors_full[0:1]), reorder(vectors_full[1:2])
    bias_at = (tp_index * QUAD + place) * att_width
    bias_here = lax.dynamic_slice_in_dim(vectors_full[2:5], bias_at, att_width, 1).reshape(1, 3 * att_width)

    own_rows, own_back = reorder(inputs[:, 0]), reorder(cotangent[:, 0])
    rows_quad, last = gather_line(own_rows, place)
    rows_quad = rows_quad.reshape(-1, depth)
    rows_other = swap(rows_quad, "tp")
    hidden_weights = [gather_weight(functools.partial(hidden_piece, part)) for part in range(parts)]
    back_quad, last = gather_line(after(own_back, last), place)
    back_quad = back_quad.reshape(-1, depth)
    back_all = jnp.concatenate([back_quad, swap(back_quad, "tp")], axis=0)
    normed, xhat_all = norm_rows(rows_quad, rows_other, row_gain, row_shift)
    tokens = normed.shape[0]

    def hidden(weight):
        gate_up = nn(normed, weight[:, : 2 * ff_part])
        act_grad = nn(back_all, weight[:, 2 * ff_part :])
        gate, up = gate_up[:, :ff_part], gate_up[:, ff_part:]
        sigma = 1.0 / (1.0 + jnp.exp(-gate))
        silu = gate * sigma
        activated = (silu * up).astype(LOW)
        gate_grad = (act_grad * up * sigma * (1.0 + gate * (1.0 - sigma))).astype(LOW)
        up_grad = (act_grad * silu).astype(LOW)
        gated_grad = jnp.concatenate([gate_grad, up_grad], axis=1)
        term = jnp.concatenate(
            [tn(normed, gated_grad).astype(LOW), tn(back_all, activated).astype(LOW)], axis=1
        )
        return activated, gated_grad, term

    joined_out = nn(normed, attention_weight[:, : 3 * att_width])
    mixed_grad = nn(back_all, attention_weight[:, 3 * att_width :]).astype(LOW)
    mixed, joined_grad, bias_grad = attention(joined_out, mixed_grad, bias_here, tp_index)
    attention_term = jnp.concatenate(
        [tn(normed, joined_grad).astype(LOW), tn(back_all, mixed).astype(LOW)], axis=1
    )
    done = [hidden(weight) for weight in hidden_weights]

    out_part = product_sum(
        [(mixed, attention_weight, 3)]
        + [(item[0], weight, 2) for item, weight in zip(done, hidden_weights)],
        tokens,
        depth,
    )
    normed_grad_part, sums = product_sum(
        [(joined_grad, attention_weight, 0)]
        + [(item[1], weight, 0) for item, weight in zip(done, hidden_weights)],
        tokens,
        depth,
        (xhat_all,),
    )

    def collect(term):
        folded = after(term).reshape(quads, QUAD, rows_here, term.shape[1])
        mine = lax.psum_scatter(folded, "p", scatter_dimension=0)
        return lax.all_to_all(mine, "a", 0, 0, tiled=True).astype(F32)

    attention_own = collect(attention_term)
    hidden_own = [collect(item[2]) for item in done]

    def scatter_rows(part):
        halves = part.reshape(2, QUAD, MICRO, 128, depth)
        quad = add_low(halves[0], swap(halves[1], "tp"))
        return scatter_line([quad[k] for k in range(QUAD)])

    branch = scatter_rows(out_part)
    own_grad = scatter_rows(normed_grad_part)
    own_float = own_rows.astype(F32)
    outputs = restore((own_float + branch).astype(LOW))[:, None]

    average = jnp.mean(own_float, axis=-1, keepdims=True)
    centred_own = own_float - average
    inverse_own = lax.rsqrt(jnp.mean(centred_own * centred_own, axis=-1, keepdims=True) + EPS_NORM)
    xhat = centred_own * inverse_own
    scaled = own_grad * row_gain
    rows_grad = inverse_own * (
        scaled
        - jnp.mean(scaled, axis=-1, keepdims=True)
        - xhat * jnp.mean(scaled * xhat, axis=-1, keepdims=True)
    )
    input_grad = restore((own_back.astype(F32) + rows_grad).astype(LOW))[:, None]

    bias_wide = lax.dynamic_update_slice(
        jnp.zeros((3, depth), F32), bias_grad.reshape(3, att_width), (0, bias_at)
    )
    vectors_term = jnp.concatenate(
        [restore(jnp.sum(sums.reshape(2, 8, depth), axis=1)), bias_wide], axis=0
    )
    vectors_grad = lax.dynamic_slice_in_dim(
        sum_small(vectors_term), (place * quads + at_p) * rows_here, rows_here, 1
    )

    def columns(piece, c):
        return piece[:, :, c * att_width : (c + 1) * att_width]

    def widen(cut):
        return jnp.concatenate([cut[index] for index in range(QUAD)], axis=1)

    joined_grads = jnp.stack([widen(columns(attention_own, c)) for c in range(3)])
    outward_grads = widen(columns(attention_own, 3))

    def hidden_columns(c):
        found = []
        for index in range(QUAD):
            for part in range(parts):
                size = min(lengths[index] - part * ff_part, ff_part)
                found.append(hidden_own[part][index][:, c * ff_part : c * ff_part + size])
        return jnp.concatenate(found, axis=1)

    gated_grads = jnp.stack([hidden_columns(0), hidden_columns(1)])
    downward_grads = hidden_columns(2)

    square = (
        sum(jnp.sum(own * own) for own in hidden_own)
        + jnp.sum(attention_own * attention_own)
        + jnp.sum(vectors_grad * vectors_grad) / tp_count
    )
    grad_norm = jnp.sqrt(sum_small(jnp.full((8, 128), square))[0, 0])
    factor = jnp.minimum(1.0, CLIP / (grad_norm + 1e-06))
    ff_total = ff_here * tp_count
    return (
        outputs,
        input_grad,
        grad_norm,
        *adamw(joined_master, joined_first, joined_second, joined_grads, factor, depth ** (-0.5), DECAY),
        *adamw(outward_master, outward_first, outward_second, outward_grads, factor, (depth // 32) ** (-0.5), DECAY),
        *adamw(gated_master, gated_first, gated_second, gated_grads, factor, depth ** (-0.5), DECAY),
        *adamw(downward_master, downward_first, downward_second, downward_grads, factor, ff_total ** (-0.5), DECAY),
        *adamw(vectors_master, vectors_first, vectors_second, vectors_grad, factor, SMALL_RATE, 0.0),
    )


def solution(mesh):
    fsdp, tp = mesh.shape["fsdp"], mesh.shape["tp"]
    fine = Mesh(mesh.devices.reshape(QUAD, fsdp // QUAD, tp), ("a", "p", "tp"))
    every = ("a", "p")
    rows = P(None, every, "tp", None)
    stacked = P(None, every, "tp")
    flat = P(every, "tp")
    vectors = P(None, every)
    return jax.shard_map(
        on_device,
        mesh=fine,
        in_specs=(rows,) * 2 + (stacked,) * 3 + (flat,) * 3 + (stacked,) * 3 + (flat,) * 3 + (vectors,) * 3,
        out_specs=(rows,) * 2
        + (P(),)
        + (stacked,) * 4
        + (flat,) * 4
        + (stacked,) * 4
        + (flat,) * 4
        + (vectors,) * 4,
        check_vma=False,
    )
```

```python
import functools
import jax
import jax.numpy as jnp
from jax import lax
from jax.experimental import pallas as pl
from jax.experimental.pallas import tpu as pltpu
from jax.sharding import Mesh
from jax.sharding import PartitionSpec as P

HD = 64
ROT = 16
MICRO = 2
STEP = 5
QUAD = 4

EPS_NORM = 1e-05
CLIP = 1.0
BETA_ONE = 0.5
BETA_TWO = 0.5
ADAM_EPS = 1e-08
DECAY = 0.1
SMALL_RATE = 0.2
ROPE_BASE = 10000.0
LOW = jnp.bfloat16
F32 = jnp.float32
SWAP = [(0, 1), (1, 0)]


def nn(left, right):
    return lax.dot_general(left, right, (((1,), (0,)), ((), ())), preferred_element_type=F32)


def nt(left, right):
    return lax.dot_general(left, right, (((1,), (1,)), ((), ())), preferred_element_type=F32)


def tn(left, right):
    return lax.dot_general(left, right, (((0,), (0,)), ((), ())), preferred_element_type=F32)


def swap(value, axis):
    return lax.ppermute(value, axis, SWAP)


ANYWHERE = pl.BlockSpec(memory_space=pl.ANY)
BIG = 56 * 1024 * 1024


def launch(kernel, name, grid, operands, in_specs, out_specs, out_shape, flops, deps=(), lead=(), aliases=None):
    count, extra, ahead = len(operands), len(deps), len(lead)

    def run(*refs):
        refs = refs[ahead:]
        kernel(*refs[:count], *refs[count + extra :])

    shapes = out_shape if isinstance(out_shape, list) else [out_shape]
    moved = sum(v.size * v.dtype.itemsize for v in operands)
    moved += sum(s.size * s.dtype.itemsize for s in shapes)
    return pl.pallas_call(
        run,
        grid_spec=pltpu.PrefetchScalarGridSpec(
            num_scalar_prefetch=ahead,
            grid=grid,
            in_specs=list(in_specs) + [ANYWHERE] * extra,
            out_specs=out_specs,
        ),
        out_shape=out_shape,
        input_output_aliases={len(lead) + k: v for k, v in (aliases or {}).items()},
        cost_estimate=pl.CostEstimate(flops=flops, bytes_accessed=moved, transcendentals=0),
        compiler_params=pltpu.CompilerParams(vmem_limit_bytes=BIG),
        name=name,
    )(*lead, *operands, *deps)


def gate_kernel(*refs):
    pass


def after(value, *others):
    if not others:
        return value
    return pl.pallas_call(
        gate_kernel,
        in_specs=[ANYWHERE] * (1 + len(others)),
        out_specs=ANYWHERE,
        out_shape=jax.ShapeDtypeStruct(value.shape, value.dtype),
        input_output_aliases={0: 0},
        name="after",
    )(value, *others)


def blank(shape, dtype):
    return pl.pallas_call(
        gate_kernel,
        out_specs=ANYWHERE,
        out_shape=jax.ShapeDtypeStruct(shape, dtype),
        name="blank",
    )()


def held(values, gate):
    return [after(value, *gate) for value in values]


def exchange(blocks, gate):
    out = held(blocks[1:], gate)
    return [blocks[0]] + [
        lax.ppermute(block, "a", [(i, i ^ bit) for i in range(QUAD)])
        for bit, block in enumerate(out, 1)
    ]


class Plane:
    def __init__(self):
        self.square = lax.axis_size("x") == 2
        self.count = lax.axis_size("x") * lax.axis_size("y")
        self.at = lax.axis_index(("y", "x"))

    def gather_first(self, mine, gate):
        if not self.square:
            return (mine,)
        to_x, to_y = held([mine, mine], gate)
        return (mine, swap(to_x, "x"), swap(to_y, "y"))

    def gather_second(self, known, gate):
        mine = known[0]
        if not self.square:
            return lax.all_gather(mine, ("y", "x"), axis=1, tiled=True), ()
        half = QUAD // 2
        upper, lower = held([known[1][:half], known[2][half:]], gate)
        last = (swap(upper, "y"), swap(lower, "x"))
        rows = mine.shape[1]
        whole = blank((QUAD, self.count * rows, mine.shape[2]), mine.dtype)
        for bits, block, first in (
            (0, mine, 0),
            (1, known[1], 0),
            (2, known[2], 0),
            (3, last[0], 0),
            (3, last[1], half),
        ):
            at = jnp.bitwise_xor(self.at, bits) * rows
            whole = lax.dynamic_update_slice(whole, block, (first, at, 0))
        return whole, last

    def part(self, term, bits):
        rows = term.shape[1] // self.count
        return lax.dynamic_slice_in_dim(term, jnp.bitwise_xor(self.at, bits) * rows, rows, 1)

    def sum_first(self, term, gate):
        if not self.square:
            return (term,)
        half = QUAD // 2
        across = self.part(term, 3)
        upper, lower = held([across[:half], across[half:]], gate)
        return (term, swap(upper, "y"), swap(lower, "x"))

    def sum_second(self, known, gate):
        term = known[0]
        if not self.square:
            return lax.psum_scatter(term, ("y", "x"), scatter_dimension=1, tiled=True), ()
        half = QUAD // 2
        to_x, to_y = self.part(term, 1), self.part(term, 2)
        to_x = jnp.concatenate([add_low(to_x[:half], known[1]), to_x[half:]])
        to_y = jnp.concatenate([to_y[:half], add_low(to_y[half:], known[2])])
        to_x, to_y = held([to_x, to_y], gate)
        last = (swap(to_x, "x"), swap(to_y, "y"))
        total = self.part(term, 0).astype(F32) + last[0].astype(F32) + last[1].astype(F32)
        return total, last


def add_low(left, right):
    return (left.astype(F32) + right.astype(F32)).astype(LOW)


def bits(axis):
    found, bit = [], 1
    count, at = lax.axis_size(axis), lax.axis_index(axis)
    while bit < count:
        found.append((axis, [(i, i ^ bit) for i in range(count)], (at // bit) % 2))
        bit *= 2
    return found


def gather_small(value):
    for axis, pairs, bit in bits("x") + bits("y") + bits("a"):
        other = lax.ppermute(value, axis, pairs)
        value = jnp.where(
            bit == 0,
            jnp.concatenate([value, other], axis=-1),
            jnp.concatenate([other, value], axis=-1),
        )
    return value


def sum_small(value):
    for axis, pairs, bit in bits("tp") + bits("x") + bits("y") + bits("a"):
        value = value + lax.ppermute(value, axis, pairs)
    return value


def attention_kernel(
    mask_ref, cos_ref, left_ref, right_ref, bias_ref, joined_ref, back_ref, mixed_ref, grad_ref, bias_grad_ref
):
    rows, width = cos_ref.shape
    heads = width // HD
    scale = HD ** (-0.5)
    joined = joined_ref[...].reshape(rows, 3 * width) + bias_ref[0:1, :]
    cos, left, right = cos_ref[...], left_ref[...], right_ref[...]

    def turn(v):
        return v * cos + pltpu.roll(v, width - ROT // 2, 1) * left + pltpu.roll(v, ROT // 2, 1) * right

    def turn_back(g):
        return g * cos - (pltpu.roll(g, width - ROT // 2, 1) * left + pltpu.roll(g, ROT // 2, 1) * right)

    query = turn(joined[:, :width]).astype(LOW)
    keys = turn(joined[:, width : 2 * width]).astype(LOW)
    values = joined[:, 2 * width :].astype(LOW)
    back = back_ref[...].reshape(rows, width)
    mask = mask_ref[...]
    mixed, d_query, d_keys, d_values = [], [], [], []
    for head in range(heads):
        cut = slice(head * HD, (head + 1) * HD)
        q, k, v, g = query[:, cut], keys[:, cut], values[:, cut], back[:, cut]
        scores = nt(q, k) * scale + mask
        peak = jnp.max(scores, axis=-1, keepdims=True)
        raised = jnp.exp(scores - peak)
        full = raised / jnp.sum(raised, axis=-1, keepdims=True)
        probs = full.astype(LOW)
        mixed.append(nn(probs, v))
        prob_grad = nt(g, v)
        weighted = full * prob_grad
        inner = jnp.sum(weighted, axis=-1, keepdims=True)
        score_grad = (weighted - full * inner).astype(LOW)
        d_query.append(nn(score_grad, k) * scale)
        d_keys.append(tn(score_grad, q) * scale)
        d_values.append(tn(probs, g))
    mixed_ref[...] = jnp.concatenate(mixed, axis=-1).astype(LOW).reshape(mixed_ref.shape)
    out = jnp.concatenate(
        [
            turn_back(jnp.concatenate(d_query, axis=-1)),
            turn_back(jnp.concatenate(d_keys, axis=-1)),
            jnp.concatenate(d_values, axis=-1),
        ],
        axis=-1,
    ).astype(LOW)
    grad_ref[...] = out.reshape(grad_ref.shape)

    @pl.when(pl.program_id(0) == 0)
    def _():
        bias_grad_ref[...] = jnp.zeros_like(bias_grad_ref)

    sums = jnp.sum(out.astype(F32).reshape(rows // 8, 8, 3 * width), axis=0)
    bias_grad_ref[...] += sums


def attention(joined, back, bias):
    tokens, width = back.shape
    half = 128
    seqs = tokens // (2 * half)
    length = 2 * half
    position = jnp.arange(length)
    mask = jnp.where(position[:, None] >= position[None, :], 0.0, -jnp.inf).astype(F32)
    frequency = ROPE_BASE ** (-(2.0 * jnp.arange(ROT // 2, dtype=F32)) / ROT)
    angles = position.astype(F32)[:, None] * frequency[None, :]
    cosine, sine = jnp.cos(angles), jnp.sin(angles)
    rest = jnp.ones((length, HD - ROT), F32)
    nothing = jnp.zeros((length, ROT // 2), F32)
    heads = width // HD
    cos = jnp.tile(jnp.concatenate([cosine, cosine, rest], 1), (1, heads))
    left = jnp.tile(jnp.concatenate([-sine, nothing, 0.0 * rest], 1), (1, heads))
    right = jnp.tile(jnp.concatenate([nothing, sine, 0.0 * rest], 1), (1, heads))
    fixed = lambda i: (0, 0)
    rows = lambda i: (i // MICRO, 0, i % MICRO, 0, 0)
    shape = lambda w: (seqs // MICRO, 2, MICRO, half, w)
    mixed, grad, bias_grad = pl.pallas_call(
        attention_kernel,
        grid=(seqs,),
        in_specs=[
            pl.BlockSpec((length, length), fixed),
            pl.BlockSpec((length, width), fixed),
            pl.BlockSpec((length, width), fixed),
            pl.BlockSpec((length, width), fixed),
            pl.BlockSpec((1, 3 * width), fixed),
            pl.BlockSpec((1, 2, 1, half, 3 * width), rows),
            pl.BlockSpec((1, 2, 1, half, width), rows),
        ],
        out_specs=[
            pl.BlockSpec((1, 2, 1, half, width), rows),
            pl.BlockSpec((1, 2, 1, half, 3 * width), rows),
            pl.BlockSpec((8, 3 * width), fixed),
        ],
        out_shape=[
            jax.ShapeDtypeStruct(shape(width), LOW),
            jax.ShapeDtypeStruct(shape(3 * width), LOW),
            jax.ShapeDtypeStruct((8, 3 * width), F32),
        ],
        cost_estimate=pl.CostEstimate(
            flops=seqs * heads * 7 * 2 * length * length * HD * 4,
            bytes_accessed=tokens * width * 30,
            transcendentals=seqs * heads * length * length,
        ),
        compiler_params=pltpu.CompilerParams(vmem_limit_bytes=32 * 1024 * 1024),
        name="attention_both_ways",
    )(mask, cos, left, right, bias, joined.reshape(shape(3 * width)), back.reshape(shape(width)))
    return (
        mixed.reshape(tokens, width),
        grad.reshape(tokens, 3 * width),
        jnp.sum(bias_grad, axis=0),
    )


def norm_kernel(gain_ref, shift_ref, rows_ref, normed_ref, xhat_ref):
    rows = rows_ref[...].astype(F32)
    average = jnp.mean(rows, axis=-1, keepdims=True)
    centred = rows - average
    variance = jnp.mean(centred * centred, axis=-1, keepdims=True)
    xhat = centred * lax.rsqrt(variance + EPS_NORM)
    xhat_ref[...] = xhat.astype(LOW)
    normed_ref[...] = (xhat * gain_ref[...] + shift_ref[...]).astype(LOW)


def by_row(i):
    return (i, 0)


def fixed(*grid):
    return (0, 0)


def norm_rows(rows, gain, shift, deps=()):
    tokens, depth = rows.shape
    tall = 256
    return launch(
        norm_kernel,
        "norm_rows",
        (tokens // tall,),
        [gain, shift, rows],
        [pl.BlockSpec((1, depth), fixed)] * 2 + [pl.BlockSpec((tall, depth), by_row)],
        [pl.BlockSpec((tall, depth), by_row)] * 2,
        [jax.ShapeDtypeStruct((tokens, depth), LOW)] * 2,
        20 * tokens * depth,
        deps,
    )


def columns_of(weight, at, width):
    return pl.BlockSpec((weight.shape[0], width), lambda i: (0, at))


def times_kernel(rows_ref, weight_ref, out_ref):
    out_ref[...] = nn(rows_ref[...], weight_ref[...]).astype(out_ref.dtype)


def times(rows, weight, at, width, dtype, deps=()):
    tokens, depth = rows.shape
    tall = 512
    return launch(
        times_kernel,
        "times",
        (tokens // tall,),
        [rows, weight],
        [pl.BlockSpec((tall, depth), by_row), columns_of(weight, at, width)],
        pl.BlockSpec((tall, width), by_row),
        jax.ShapeDtypeStruct((tokens, width), dtype),
        2 * tokens * depth * width,
        deps,
    )


def gate_up_kernel(rows_ref, weight_ref, act_ref, silu_ref, slope_ref):
    width = silu_ref.shape[1]
    both = nn(rows_ref[...], weight_ref[...])
    gate, up = both[:, :width], both[:, width:]
    sigma = 1.0 / (1.0 + jnp.exp(-gate))
    silu = gate * sigma
    act_ref[...] = (silu * up).astype(LOW)
    silu_ref[...] = silu
    slope_ref[...] = up * sigma * (1.0 + gate * (1.0 - sigma))


def gate_up(rows, weight, deps=()):
    tokens, depth = rows.shape
    width = weight.shape[1] // 2
    tall = 512
    return launch(
        gate_up_kernel,
        "gate_up",
        (tokens // tall,),
        [rows, weight],
        [pl.BlockSpec((tall, depth), by_row), pl.BlockSpec(weight.shape, fixed)],
        [pl.BlockSpec((tall, width), by_row)] * 3,
        [jax.ShapeDtypeStruct((tokens, width), dtype) for dtype in (LOW, F32, F32)],
        4 * tokens * depth * width,
        deps,
    )


def gate_up_back_kernel(rows_ref, weight_ref, silu_ref, slope_ref, out_ref):
    width = silu_ref.shape[1]
    act_grad = nn(rows_ref[...], weight_ref[...])
    out_ref[:, :width] = (act_grad * slope_ref[...]).astype(LOW)
    out_ref[:, width:] = (act_grad * silu_ref[...]).astype(LOW)


def gate_up_back(rows, weight, silu, slope, deps=()):
    tokens, depth = rows.shape
    width = weight.shape[1]
    tall = 512
    return launch(
        gate_up_back_kernel,
        "gate_up_back",
        (tokens // tall,),
        [rows, weight, silu, slope],
        [pl.BlockSpec((tall, depth), by_row), pl.BlockSpec(weight.shape, fixed)]
        + [pl.BlockSpec((tall, width), by_row)] * 2,
        pl.BlockSpec((tall, 2 * width), by_row),
        jax.ShapeDtypeStruct((tokens, 2 * width), LOW),
        2 * tokens * depth * width,
        deps,
    )


def term_kernel(*refs):
    out_ref = refs[-1]
    at = 0
    for grads_ref, rows_ref in zip(refs[0:-1:2], refs[1:-1:2]):
        width = grads_ref.shape[1]
        out_ref[:, at : at + width] = tn(rows_ref[...], grads_ref[...]).astype(LOW)
        at += width


def weight_term(items, deps=()):
    operands, in_specs = [], []
    broad = 512
    for grads, rows in items:
        operands += [grads, rows]
        in_specs.append(pl.BlockSpec(grads.shape, fixed))
        in_specs.append(pl.BlockSpec((rows.shape[0], broad), lambda j: (0, j)))
    tokens, depth = rows.shape
    width = sum(grads.shape[1] for grads, _ in items)
    return launch(
        term_kernel,
        "weight_term",
        (depth // broad,),
        operands,
        in_specs,
        pl.BlockSpec((broad, width), by_row),
        jax.ShapeDtypeStruct((depth, width), LOW),
        2 * tokens * depth * width,
        deps,
    )


def product_kernel(terms, with_xhat, *refs):
    lefts, rights, rest = refs[:terms], refs[terms : 2 * terms], refs[2 * terms :]
    total = nt(lefts[0][...], rights[0][...])
    for left, right in zip(lefts[1:], rights[1:]):
        total += nt(left[...], right[...])
    if not with_xhat:
        rest[-1][...] = total.astype(LOW)
        return
    xhat_ref, out_ref, sums_ref = rest[0], rest[-2], rest[-1]
    out_ref[...] = total.astype(LOW)
    xhat = xhat_ref[...].astype(F32)

    @pl.when(pl.program_id(0) == 0)
    def _():
        sums_ref[...] = jnp.zeros_like(sums_ref)

    tall = total.shape[0] // 8
    sums_ref[0:8, :] += jnp.sum((total * xhat).reshape(tall, 8, -1), axis=0)
    sums_ref[8:16, :] += jnp.sum(total.reshape(tall, 8, -1), axis=0)


def product_sum(pairs, depth, xhat=None, deps=(), part=None, into=None):
    tall = 512
    terms = len(pairs)
    rows = pairs[0][0].shape[0]
    steps = rows // tall if part is None else rows // tall // 2
    first = steps * (part or 0)
    below = lambda i: (i + first, 0)
    in_specs = [pl.BlockSpec((tall, left.shape[1]), below) for left, _, _ in pairs]
    in_specs += [columns_of(right, at, left.shape[1]) for left, right, at in pairs]
    operands = [p[0] for p in pairs] + [p[1] for p in pairs]
    out_specs = [pl.BlockSpec((tall, depth), below)]
    out_shape = [jax.ShapeDtypeStruct((rows, depth), LOW)]
    if xhat is not None:
        in_specs.append(pl.BlockSpec((tall, depth), below))
        operands.append(xhat)
        out_specs.append(pl.BlockSpec((16, depth), fixed))
        out_shape.append(jax.ShapeDtypeStruct((16, depth), F32))
    aliases = {}
    if into is not None:
        aliases = {len(operands): 0}
        in_specs.append(ANYWHERE)
        operands.append(into)
    deep = sum(left.shape[1] for left, _, _ in pairs)
    found = launch(
        functools.partial(product_kernel, terms, xhat is not None),
        "product_sum",
        (steps,),
        operands,
        in_specs,
        out_specs,
        out_shape,
        2 * steps * tall * depth * deep,
        deps,
        (),
        aliases,
    )
    return found if xhat is not None else (found[0], None)


def adamw(master, first_old, second_old, gradient, factor, step_rate, weight_decay):
    clipped = gradient * factor
    moment = BETA_ONE * first_old + (1.0 - BETA_ONE) * clipped
    variance = BETA_TWO * second_old + (1.0 - BETA_TWO) * clipped * clipped
    moment_hat = moment / (1.0 - BETA_ONE**STEP)
    variance_hat = variance / (1.0 - BETA_TWO**STEP)
    updated = master - step_rate * (
        moment_hat / (jnp.sqrt(variance_hat) + ADAM_EPS) + weight_decay * master
    )
    return (updated, moment, variance, updated.astype(LOW))


def on_device(
    inputs,
    cotangent,
    joined_master,
    joined_first,
    joined_second,
    outward_master,
    outward_first,
    outward_second,
    gated_master,
    gated_first,
    gated_second,
    downward_master,
    downward_first,
    downward_second,
    vectors_master,
    vectors_first,
    vectors_second,
):
    tp_count = lax.axis_size("tp")
    plane = Plane()
    place = lax.axis_index("a")
    tp_index = lax.axis_index("tp")
    depth = inputs.shape[-1]
    rows_here = joined_master.shape[1]
    att_width = joined_master.shape[2] // QUAD
    ff_here = gated_master.shape[2]
    tiles = ff_here // 128
    wide = -(-tiles // QUAD)
    ff_width = wide * 128
    shortage = wide * QUAD - tiles

    lacking = QUAD - shortage
    firsts = [index * wide - max(0, index - lacking) for index in range(QUAD)]
    skips = [(first - min(first, tiles - wide)) * 128 for first in firsts]
    lengths = [(wide - (index >= lacking)) * 128 for index in range(QUAD)]

    def attention_piece(index):
        cut = lambda w: lax.dynamic_slice_in_dim(w, index * att_width, att_width, 1)
        return jnp.concatenate(
            [cut(joined_master[c]) for c in range(3)] + [cut(outward_master)], axis=1
        ).astype(LOW)

    def hidden_cut(w, index):
        first = index * wide - jnp.maximum(0, index - lacking)
        start = jnp.minimum(first, tiles - wide)
        skip = (first - start) * 128
        length = jnp.where(index >= lacking, wide - 1, wide) * 128
        column = lax.broadcasted_iota(jnp.int32, (1, ff_width), 1)
        keep = (column >= skip) & (column < skip + length)
        part = lax.dynamic_slice_in_dim(w, start * 128, ff_width, 1)
        return jnp.where(keep, part, 0.0).astype(LOW)

    def gated_piece(index):
        return jnp.concatenate([hidden_cut(gated_master[c], index) for c in range(2)], axis=1)

    def downward_piece(index):
        return hidden_cut(downward_master, index)

    def other(bit):
        return jnp.bitwise_xor(place, bit)

    def pieces(make):
        return [make(other(bits)) for bits in range(QUAD)]

    def ordered(blocks):
        stacked = jnp.stack(blocks)
        return jnp.stack(
            [lax.dynamic_index_in_dim(stacked, other(j), 0, False) for j in range(QUAD)]
        )

    vectors_low = gather_small(vectors_master.astype(LOW))
    vectors_full = vectors_low.astype(F32)
    row_gain, row_shift = vectors_full[0:1], vectors_full[1:2]
    bias_at = (tp_index * QUAD + place) * att_width
    bias_here = lax.dynamic_slice_in_dim(vectors_full[2:5], bias_at, att_width, 1).reshape(1, 3 * att_width)

    own_rows, own_back = inputs[:, 0], cotangent[:, 0]
    line = ("a", "tp")
    rows_all = lax.all_gather(own_rows, line, axis=0).reshape(-1, depth)
    back_all = lax.all_gather(own_back, line, axis=0).reshape(-1, depth)

    def flat(weight):
        return weight.reshape(depth, weight.shape[-1])

    joined = exchange(pieces(attention_piece), (vectors_low,))
    joined_near = plane.gather_first(ordered(joined), joined[1:])
    gated = exchange(pieces(gated_piece), joined[1:])
    stage = [*joined_near[1:], *gated[1:], rows_all]
    gated_near = plane.gather_first(ordered(gated), stage)
    downward = exchange(pieces(downward_piece), stage)
    normed, xhat_all = norm_rows(rows_all, row_gain, row_shift)
    stage = [*gated_near[1:], *downward[1:], normed]
    gated_weight, last = plane.gather_second(gated_near, stage)
    gated_weight = flat(gated_weight)
    downward_near = plane.gather_first(ordered(downward), stage)
    stage = [*last, *downward_near[1:]]
    attention_weight, joined_last = plane.gather_second(joined_near, stage)
    attention_weight = flat(attention_weight)
    downward_weight, last = plane.gather_second(downward_near, stage)
    downward_weight = flat(downward_weight)
    activated, silu, slope = gate_up(normed, gated_weight)
    joined_out = times(normed, attention_weight, 0, 3 * att_width, F32, (activated, *last))
    downward_term = weight_term([(activated, back_all)], (joined_out,))
    mixed_grad = times(back_all, attention_weight, 3, att_width, LOW, (downward_term,))
    mixed, joined_grad, bias_grad = attention(joined_out, mixed_grad, bias_here)

    def fold(term):
        return term.reshape(QUAD, depth // QUAD, term.shape[1])

    def homeward(total, gate):
        total = total.astype(LOW)
        return exchange(
            [lax.dynamic_index_in_dim(total, other(bits), 0, False) for bits in range(QUAD)], gate
        )

    def scatter_rows(part):
        folded = part.reshape(2 * QUAD, MICRO, 128, depth)
        return lax.psum_scatter(folded, line, scatter_dimension=0)

    downward_total = lax.psum_scatter(
        fold(downward_term), ("y", "x"), scatter_dimension=1, tiled=True
    )
    out_part, _ = product_sum([(mixed, attention_weight, 3), (activated, downward_weight, 0)], depth)
    branch = scatter_rows(out_part)
    attention_term = weight_term([(joined_grad, normed), (mixed, back_all)], (out_part,))
    joined_known = plane.sum_first(fold(attention_term), ())
    gated_grad = gate_up_back(back_all, downward_weight, silu, slope, (attention_term,))
    gated_term = weight_term([(gated_grad, normed)], joined_known[1:])
    joined_total, last = plane.sum_second(joined_known, joined_known[1:])
    downward_home = homeward(downward_total, joined_known[1:])
    grad_pairs = [(joined_grad, attention_weight, 0), (gated_grad, gated_weight, 0)]
    half_done, sums_low = product_sum(grad_pairs, depth, xhat_all, (gated_term, *last), 0)
    joined_home = homeward(joined_total, last)
    gated_known = plane.sum_first(fold(gated_term), last)
    normed_grad_part, sums_high = product_sum(
        grad_pairs, depth, xhat_all, (*downward_home[1:], *gated_known[1:]), 1, half_done
    )
    gated_total, last = plane.sum_second(gated_known, gated_known[1:])
    own_grad = scatter_rows(after(normed_grad_part, branch, *joined_home[1:], *last)).astype(F32)
    gated_home = homeward(gated_total, [*last, *joined_home[1:]])
    sums = sums_low + sums_high
    branch = branch.astype(F32)

    def settled(home):
        return [block.astype(F32) for block in ordered(home)]

    downward_own, attention_own, gated_own = settled(downward_home), settled(joined_home), settled(gated_home)

    own_float = own_rows.astype(F32)
    outputs = (own_float + branch).astype(LOW)[:, None]
    average = jnp.mean(own_float, axis=-1, keepdims=True)
    centred_own = own_float - average
    inverse_own = lax.rsqrt(jnp.mean(centred_own * centred_own, axis=-1, keepdims=True) + EPS_NORM)
    xhat = centred_own * inverse_own
    scaled = own_grad * row_gain
    rows_grad = inverse_own * (
        scaled
        - jnp.mean(scaled, axis=-1, keepdims=True)
        - xhat * jnp.mean(scaled * xhat, axis=-1, keepdims=True)
    )
    input_grad = (own_back.astype(F32) + rows_grad).astype(LOW)[:, None]

    bias_wide = lax.dynamic_update_slice(
        jnp.zeros((3, depth), F32), bias_grad.reshape(3, att_width), (0, bias_at)
    )
    sums = jnp.sum(sums.reshape(2, 8, depth), axis=1)
    vectors_term = after(jnp.concatenate([sums, bias_wide], axis=0), *last)
    vectors_sum = sum_small(vectors_term)
    vectors_grad = lax.dynamic_slice_in_dim(
        vectors_sum, (place * plane.count + plane.at) * rows_here, rows_here, 1
    )

    def attention_columns(c):
        cut = slice(c * att_width, (c + 1) * att_width)
        return jnp.concatenate([piece[:, cut] for piece in attention_own], axis=1)

    joined_grads = jnp.stack([attention_columns(c) for c in range(3)])
    outward_grads = attention_columns(3)

    def hidden_columns(pieces, c):
        return jnp.concatenate(
            [
                piece[:, c * ff_width + skip : c * ff_width + skip + length]
                for piece, skip, length in zip(pieces, skips, lengths)
            ],
            axis=1,
        )

    gated_grads = jnp.stack([hidden_columns(gated_own, c) for c in range(2)])
    downward_grads = hidden_columns(downward_own, 0)

    square = sum(jnp.sum(own * own) for own in downward_own + attention_own + gated_own)
    square = sum_small(jnp.full((8, 128), square))[0, 0] + jnp.sum(vectors_sum * vectors_sum)
    grad_norm = jnp.sqrt(square)
    factor = jnp.minimum(1.0, CLIP / (grad_norm + 1e-06))
    ff_total = ff_here * tp_count
    return (
        outputs,
        input_grad,
        grad_norm,
        *adamw(joined_master, joined_first, joined_second, joined_grads, factor, depth ** (-0.5), DECAY),
        *adamw(outward_master, outward_first, outward_second, outward_grads, factor, (depth // 32) ** (-0.5), DECAY),
        *adamw(gated_master, gated_first, gated_second, gated_grads, factor, depth ** (-0.5), DECAY),
        *adamw(downward_master, downward_first, downward_second, downward_grads, factor, ff_total ** (-0.5), DECAY),
        *adamw(vectors_master, vectors_first, vectors_second, vectors_grad, factor, SMALL_RATE, 0.0),
    )


def solution(mesh):
    fsdp, tp = mesh.shape["fsdp"], mesh.shape["tp"]
    fine = Mesh(mesh.devices.reshape(QUAD, 2, fsdp // QUAD // 2, tp), ("a", "y", "x", "tp"))
    every = ("a", "y", "x")
    rows = P(None, every, "tp", None)
    stacked = P(None, every, "tp")
    flat = P(every, "tp")
    vectors = P(None, every)
    return jax.shard_map(
        on_device,
        mesh=fine,
        in_specs=(rows,) * 2 + (stacked,) * 3 + (flat,) * 3 + (stacked,) * 3 + (flat,) * 3 + (vectors,) * 3,
        out_specs=(rows,) * 2
        + (P(),)
        + (stacked,) * 4
        + (flat,) * 4
        + (stacked,) * 4
        + (flat,) * 4
        + (vectors,) * 4,
        check_vma=False,
    )
```

```python
import functools
import jax
import jax.numpy as jnp
from jax import lax
from jax.experimental import pallas as pl
from jax.experimental.pallas import tpu as pltpu
from jax.sharding import Mesh
from jax.sharding import PartitionSpec as P

HD = 64
ROT = 16
MICRO = 2
STEP = 5
QUAD = 4

EPS_NORM = 1e-05
CLIP = 1.0
BETA_ONE = 0.5
BETA_TWO = 0.5
ADAM_EPS = 1e-08
DECAY = 0.1
SMALL_RATE = 0.2
ROPE_BASE = 10000.0
LOW = jnp.bfloat16
F32 = jnp.float32
SWAP = [(0, 1), (1, 0)]


def nn(left, right):
    return lax.dot_general(left, right, (((1,), (0,)), ((), ())), preferred_element_type=F32)


def nt(left, right):
    return lax.dot_general(left, right, (((1,), (1,)), ((), ())), preferred_element_type=F32)


def tn(left, right):
    return lax.dot_general(left, right, (((0,), (0,)), ((), ())), preferred_element_type=F32)


def swap(value, axis):
    return lax.ppermute(value, axis, SWAP)


ANYWHERE = pl.BlockSpec(memory_space=pl.ANY)
BIG = 56 * 1024 * 1024


def launch(kernel, name, grid, operands, in_specs, out_specs, out_shape, flops, deps=(), lead=(), aliases=None):
    count, extra, ahead = len(operands), len(deps), len(lead)

    def run(*refs):
        refs = refs[ahead:]
        kernel(*refs[:count], *refs[count + extra :])

    shapes = out_shape if isinstance(out_shape, list) else [out_shape]
    moved = sum(v.size * v.dtype.itemsize for v in operands)
    moved += sum(s.size * s.dtype.itemsize for s in shapes)
    return pl.pallas_call(
        run,
        grid_spec=pltpu.PrefetchScalarGridSpec(
            num_scalar_prefetch=ahead,
            grid=grid,
            in_specs=list(in_specs) + [ANYWHERE] * extra,
            out_specs=out_specs,
        ),
        out_shape=out_shape,
        input_output_aliases={len(lead) + k: v for k, v in (aliases or {}).items()},
        cost_estimate=pl.CostEstimate(flops=flops, bytes_accessed=moved, transcendentals=0),
        compiler_params=pltpu.CompilerParams(vmem_limit_bytes=BIG),
        name=name,
    )(*lead, *operands, *deps)


def gate_kernel(*refs):
    pass


def after(value, *others):
    if not others:
        return value
    return pl.pallas_call(
        gate_kernel,
        in_specs=[ANYWHERE] * (1 + len(others)),
        out_specs=ANYWHERE,
        out_shape=jax.ShapeDtypeStruct(value.shape, value.dtype),
        input_output_aliases={0: 0},
        name="after",
    )(value, *others)


def blank(shape, dtype):
    return pl.pallas_call(
        gate_kernel,
        out_specs=ANYWHERE,
        out_shape=jax.ShapeDtypeStruct(shape, dtype),
        name="blank",
    )()


def held(values, gate):
    return [after(value, *gate) for value in values]


def exchange(blocks, gate):
    out = held(blocks[1:], gate)
    return [blocks[0]] + [
        lax.ppermute(block, "a", [(i, i ^ bit) for i in range(QUAD)])
        for bit, block in enumerate(out, 1)
    ]


class Plane:
    def __init__(self):
        self.square = lax.axis_size("x") == 2
        self.count = lax.axis_size("x") * lax.axis_size("y")
        self.at = lax.axis_index(("y", "x"))

    def gather_first(self, mine, gate):
        if not self.square:
            return (mine,)
        to_x, to_y = held([mine, mine], gate)
        return (mine, swap(to_x, "x"), swap(to_y, "y"))

    def gather_second(self, known, gate):
        mine = known[0]
        if not self.square:
            return lax.all_gather(mine, ("y", "x"), axis=1, tiled=True), ()
        half = QUAD // 2
        upper, lower = held([known[1][:half], known[2][half:]], gate)
        last = (swap(upper, "y"), swap(lower, "x"))
        rows = mine.shape[1]
        whole = blank((QUAD, self.count * rows, mine.shape[2]), mine.dtype)
        for bits, block, first in (
            (0, mine, 0),
            (1, known[1], 0),
            (2, known[2], 0),
            (3, last[0], 0),
            (3, last[1], half),
        ):
            at = jnp.bitwise_xor(self.at, bits) * rows
            whole = lax.dynamic_update_slice(whole, block, (first, at, 0))
        return whole, last

    def part(self, term, bits):
        rows = term.shape[1] // self.count
        return lax.dynamic_slice_in_dim(term, jnp.bitwise_xor(self.at, bits) * rows, rows, 1)

    def sum_first(self, term, gate):
        if not self.square:
            return (term,)
        half = QUAD // 2
        across = self.part(term, 3)
        upper, lower = held([across[:half], across[half:]], gate)
        return (term, swap(upper, "y"), swap(lower, "x"))

    def sum_second(self, known, gate):
        term = known[0]
        if not self.square:
            return lax.psum_scatter(term, ("y", "x"), scatter_dimension=1, tiled=True), ()
        half = QUAD // 2
        to_x, to_y = self.part(term, 1), self.part(term, 2)
        to_x = jnp.concatenate([add_low(to_x[:half], known[1]), to_x[half:]])
        to_y = jnp.concatenate([to_y[:half], add_low(to_y[half:], known[2])])
        to_x, to_y = held([to_x, to_y], gate)
        last = (swap(to_x, "x"), swap(to_y, "y"))
        total = self.part(term, 0).astype(F32) + last[0].astype(F32) + last[1].astype(F32)
        return total, last


def add_low(left, right):
    return (left.astype(F32) + right.astype(F32)).astype(LOW)


def bits(axis):
    found, bit = [], 1
    count, at = lax.axis_size(axis), lax.axis_index(axis)
    while bit < count:
        found.append((axis, [(i, i ^ bit) for i in range(count)], (at // bit) % 2))
        bit *= 2
    return found


def gather_small(value):
    for axis, pairs, bit in bits("x") + bits("y") + bits("a"):
        other = lax.ppermute(value, axis, pairs)
        value = jnp.where(
            bit == 0,
            jnp.concatenate([value, other], axis=-1),
            jnp.concatenate([other, value], axis=-1),
        )
    return value


def sum_small(value):
    for axis, pairs, bit in bits("tp") + bits("x") + bits("y") + bits("a"):
        value = value + lax.ppermute(value, axis, pairs)
    return value


def attention_kernel(
    mask_ref, cos_ref, left_ref, right_ref, bias_ref, joined_ref, back_ref, mixed_ref, grad_ref, bias_grad_ref
):
    rows, width = cos_ref.shape
    heads = width // HD
    scale = HD ** (-0.5)
    joined = joined_ref[...].reshape(rows, 3 * width) + bias_ref[0:1, :]
    cos, left, right = cos_ref[...], left_ref[...], right_ref[...]

    def turn(v):
        return v * cos + pltpu.roll(v, width - ROT // 2, 1) * left + pltpu.roll(v, ROT // 2, 1) * right

    def turn_back(g):
        return g * cos - (pltpu.roll(g, width - ROT // 2, 1) * left + pltpu.roll(g, ROT // 2, 1) * right)

    query = turn(joined[:, :width]).astype(LOW)
    keys = turn(joined[:, width : 2 * width]).astype(LOW)
    values = joined[:, 2 * width :].astype(LOW)
    back = back_ref[...].reshape(rows, width)
    mask = mask_ref[...]
    mixed, d_query, d_keys, d_values = [], [], [], []
    for head in range(heads):
        cut = slice(head * HD, (head + 1) * HD)
        q, k, v, g = query[:, cut], keys[:, cut], values[:, cut], back[:, cut]
        q = q * jnp.asarray(scale, LOW)
        scores = nt(q, k) + mask
        peak = jnp.max(scores, axis=-1, keepdims=True)
        raised = jnp.exp(scores - peak)
        full = raised * (1.0 / jnp.sum(raised, axis=-1, keepdims=True))
        probs = full.astype(LOW)
        mixed.append(nn(probs, v))
        prob_grad = nt(g, v)
        weighted = full * prob_grad
        inner = jnp.sum(weighted, axis=-1, keepdims=True)
        score_grad = (weighted - full * inner).astype(LOW)
        d_query.append(nn(score_grad, k) * scale)
        d_keys.append(tn(score_grad, q))
        d_values.append(tn(probs, g))
    mixed_ref[...] = jnp.concatenate(mixed, axis=-1).astype(LOW).reshape(mixed_ref.shape)
    out = jnp.concatenate(
        [
            turn_back(jnp.concatenate(d_query, axis=-1)),
            turn_back(jnp.concatenate(d_keys, axis=-1)),
            jnp.concatenate(d_values, axis=-1),
        ],
        axis=-1,
    ).astype(LOW)
    grad_ref[...] = out.reshape(grad_ref.shape)

    @pl.when(pl.program_id(0) == 0)
    def _():
        bias_grad_ref[...] = jnp.zeros_like(bias_grad_ref)

    sums = jnp.sum(out.astype(F32).reshape(rows // 8, 8, 3 * width), axis=0)
    bias_grad_ref[...] += sums


def attention(joined, back, bias, deps=()):
    tokens, width = back.shape
    half = 128
    seqs = tokens // (2 * half)
    length = 2 * half
    position = jnp.arange(length)
    mask = jnp.where(position[:, None] >= position[None, :], 0.0, -jnp.inf).astype(F32)
    frequency = ROPE_BASE ** (-(2.0 * jnp.arange(ROT // 2, dtype=F32)) / ROT)
    angles = position.astype(F32)[:, None] * frequency[None, :]
    cosine, sine = jnp.cos(angles), jnp.sin(angles)
    rest = jnp.ones((length, HD - ROT), F32)
    nothing = jnp.zeros((length, ROT // 2), F32)
    heads = width // HD
    cos = jnp.tile(jnp.concatenate([cosine, cosine, rest], 1), (1, heads))
    left = jnp.tile(jnp.concatenate([-sine, nothing, 0.0 * rest], 1), (1, heads))
    right = jnp.tile(jnp.concatenate([nothing, sine, 0.0 * rest], 1), (1, heads))
    rows = lambda i: (i // MICRO, 0, i % MICRO, 0, 0)
    shape = lambda w: (seqs // MICRO, 2, MICRO, half, w)
    mixed, grad, bias_grad = launch(
        attention_kernel,
        "attention_both_ways",
        (seqs,),
        [mask, cos, left, right, bias, joined.reshape(shape(3 * width)), back.reshape(shape(width))],
        [
            pl.BlockSpec((length, length), fixed),
            pl.BlockSpec((length, width), fixed),
            pl.BlockSpec((length, width), fixed),
            pl.BlockSpec((length, width), fixed),
            pl.BlockSpec((1, 3 * width), fixed),
            pl.BlockSpec((1, 2, 1, half, 3 * width), rows),
            pl.BlockSpec((1, 2, 1, half, width), rows),
        ],
        [
            pl.BlockSpec((1, 2, 1, half, width), rows),
            pl.BlockSpec((1, 2, 1, half, 3 * width), rows),
            pl.BlockSpec((8, 3 * width), fixed),
        ],
        [
            jax.ShapeDtypeStruct(shape(width), LOW),
            jax.ShapeDtypeStruct(shape(3 * width), LOW),
            jax.ShapeDtypeStruct((8, 3 * width), F32),
        ],
        seqs * heads * 7 * 2 * length * length * HD * 4,
        deps,
    )
    return (
        mixed.reshape(tokens, width),
        grad.reshape(tokens, 3 * width),
        jnp.sum(bias_grad, axis=0),
    )


def norm_kernel(gain_ref, shift_ref, rows_ref, normed_ref, xhat_ref):
    rows = rows_ref[...].astype(F32)
    average = jnp.mean(rows, axis=-1, keepdims=True)
    centred = rows - average
    variance = jnp.mean(centred * centred, axis=-1, keepdims=True)
    xhat = centred * lax.rsqrt(variance + EPS_NORM)
    xhat_ref[...] = xhat.astype(LOW)
    normed_ref[...] = (xhat * gain_ref[...] + shift_ref[...]).astype(LOW)


def by_row(i):
    return (i, 0)


def fixed(*grid):
    return (0, 0)


def norm_rows(rows, gain, shift, deps=()):
    tokens, depth = rows.shape
    tall = 256
    return launch(
        norm_kernel,
        "norm_rows",
        (tokens // tall,),
        [gain, shift, rows],
        [pl.BlockSpec((1, depth), fixed)] * 2 + [pl.BlockSpec((tall, depth), by_row)],
        [pl.BlockSpec((tall, depth), by_row)] * 2,
        [jax.ShapeDtypeStruct((tokens, depth), LOW)] * 2,
        20 * tokens * depth,
        deps,
    )


def columns_of(weight, at, width):
    return pl.BlockSpec((weight.shape[0], width), lambda i: (0, at))


def times_kernel(rows_ref, weight_ref, out_ref):
    out_ref[...] = nn(rows_ref[...], weight_ref[...]).astype(out_ref.dtype)


def times(rows, weight, at, width, dtype, deps=()):
    tokens, depth = rows.shape
    tall = 512
    return launch(
        times_kernel,
        "times",
        (tokens // tall,),
        [rows, weight],
        [pl.BlockSpec((tall, depth), by_row), columns_of(weight, at, width)],
        pl.BlockSpec((tall, width), by_row),
        jax.ShapeDtypeStruct((tokens, width), dtype),
        2 * tokens * depth * width,
        deps,
    )


def gate_up_kernel(rows_ref, weight_ref, act_ref, silu_ref, slope_ref):
    width = silu_ref.shape[1]
    both = nn(rows_ref[...], weight_ref[...])
    gate, up = both[:, :width], both[:, width:]
    sigma = 1.0 / (1.0 + jnp.exp(-gate))
    silu = gate * sigma
    act_ref[...] = (silu * up).astype(LOW)
    silu_ref[...] = silu
    slope_ref[...] = up * sigma * (1.0 + gate * (1.0 - sigma))


def gate_up(rows, weight, deps=()):
    tokens, depth = rows.shape
    width = weight.shape[1] // 2
    tall = 512
    return launch(
        gate_up_kernel,
        "gate_up",
        (tokens // tall,),
        [rows, weight],
        [pl.BlockSpec((tall, depth), by_row), pl.BlockSpec(weight.shape, fixed)],
        [pl.BlockSpec((tall, width), by_row)] * 3,
        [jax.ShapeDtypeStruct((tokens, width), dtype) for dtype in (LOW, F32, F32)],
        4 * tokens * depth * width,
        deps,
    )


def gate_up_back_kernel(rows_ref, weight_ref, silu_ref, slope_ref, out_ref):
    width = silu_ref.shape[1]
    act_grad = nn(rows_ref[...], weight_ref[...])
    out_ref[:, :width] = (act_grad * slope_ref[...]).astype(LOW)
    out_ref[:, width:] = (act_grad * silu_ref[...]).astype(LOW)


def gate_up_back(rows, weight, silu, slope, deps=()):
    tokens, depth = rows.shape
    width = weight.shape[1]
    tall = 512
    return launch(
        gate_up_back_kernel,
        "gate_up_back",
        (tokens // tall,),
        [rows, weight, silu, slope],
        [pl.BlockSpec((tall, depth), by_row), pl.BlockSpec(weight.shape, fixed)]
        + [pl.BlockSpec((tall, width), by_row)] * 2,
        pl.BlockSpec((tall, 2 * width), by_row),
        jax.ShapeDtypeStruct((tokens, 2 * width), LOW),
        2 * tokens * depth * width,
        deps,
    )


def term_kernel(*refs):
    out_ref = refs[-1]
    at = 0
    for grads_ref, rows_ref in zip(refs[0:-1:2], refs[1:-1:2]):
        width = grads_ref.shape[1]
        out_ref[:, at : at + width] = tn(rows_ref[...], grads_ref[...]).astype(LOW)
        at += width


def weight_term(items, deps=()):
    operands, in_specs = [], []
    broad = 512
    for grads, rows in items:
        operands += [grads, rows]
        in_specs.append(pl.BlockSpec(grads.shape, fixed))
        in_specs.append(pl.BlockSpec((rows.shape[0], broad), lambda j: (0, j)))
    tokens, depth = rows.shape
    width = sum(grads.shape[1] for grads, _ in items)
    return launch(
        term_kernel,
        "weight_term",
        (depth // broad,),
        operands,
        in_specs,
        pl.BlockSpec((broad, width), by_row),
        jax.ShapeDtypeStruct((depth, width), LOW),
        2 * tokens * depth * width,
        deps,
    )


def product_kernel(terms, with_xhat, *refs):
    lefts, rights, rest = refs[:terms], refs[terms : 2 * terms], refs[2 * terms :]
    total = nt(lefts[0][...], rights[0][...])
    for left, right in zip(lefts[1:], rights[1:]):
        total += nt(left[...], right[...])
    if not with_xhat:
        rest[-1][...] = total.astype(LOW)
        return
    xhat_ref, out_ref, sums_ref = rest[0], rest[-2], rest[-1]
    out_ref[...] = total.astype(LOW)
    xhat = xhat_ref[...].astype(F32)

    @pl.when(pl.program_id(0) == 0)
    def _():
        sums_ref[...] = jnp.zeros_like(sums_ref)

    tall = total.shape[0] // 8
    sums_ref[0:8, :] += jnp.sum((total * xhat).reshape(tall, 8, -1), axis=0)
    sums_ref[8:16, :] += jnp.sum(total.reshape(tall, 8, -1), axis=0)


def product_sum(pairs, depth, xhat=None, deps=(), part=None, into=None):
    tall = 512
    terms = len(pairs)
    rows = pairs[0][0].shape[0]
    steps = rows // tall if part is None else rows // tall // 2
    first = steps * (part or 0)
    below = lambda i: (i + first, 0)
    in_specs = [pl.BlockSpec((tall, left.shape[1]), below) for left, _, _ in pairs]
    in_specs += [columns_of(right, at, left.shape[1]) for left, right, at in pairs]
    operands = [p[0] for p in pairs] + [p[1] for p in pairs]
    out_specs = [pl.BlockSpec((tall, depth), below)]
    out_shape = [jax.ShapeDtypeStruct((rows, depth), LOW)]
    if xhat is not None:
        in_specs.append(pl.BlockSpec((tall, depth), below))
        operands.append(xhat)
        out_specs.append(pl.BlockSpec((16, depth), fixed))
        out_shape.append(jax.ShapeDtypeStruct((16, depth), F32))
    aliases = {}
    if into is not None:
        aliases = {len(operands): 0}
        in_specs.append(ANYWHERE)
        operands.append(into)
    deep = sum(left.shape[1] for left, _, _ in pairs)
    found = launch(
        functools.partial(product_kernel, terms, xhat is not None),
        "product_sum",
        (steps,),
        operands,
        in_specs,
        out_specs,
        out_shape,
        2 * steps * tall * depth * deep,
        deps,
        (),
        aliases,
    )
    return found if xhat is not None else (found[0], None)


def adamw(master, first_old, second_old, gradient, factor, step_rate, weight_decay):
    clipped = gradient * factor
    moment = BETA_ONE * first_old + (1.0 - BETA_ONE) * clipped
    variance = BETA_TWO * second_old + (1.0 - BETA_TWO) * clipped * clipped
    moment_hat = moment / (1.0 - BETA_ONE**STEP)
    variance_hat = variance / (1.0 - BETA_TWO**STEP)
    updated = master - step_rate * (
        moment_hat / (jnp.sqrt(variance_hat) + ADAM_EPS) + weight_decay * master
    )
    return (updated, moment, variance, updated.astype(LOW))


def on_device(
    inputs,
    cotangent,
    joined_master,
    joined_first,
    joined_second,
    outward_master,
    outward_first,
    outward_second,
    gated_master,
    gated_first,
    gated_second,
    downward_master,
    downward_first,
    downward_second,
    vectors_master,
    vectors_first,
    vectors_second,
):
    tp_count = lax.axis_size("tp")
    plane = Plane()
    place = lax.axis_index("a")
    tp_index = lax.axis_index("tp")
    depth = inputs.shape[-1]
    rows_here = joined_master.shape[1]
    att_width = joined_master.shape[2] // QUAD
    ff_here = gated_master.shape[2]
    tiles = ff_here // 128
    wide = -(-tiles // QUAD)
    ff_width = wide * 128
    shortage = wide * QUAD - tiles

    lacking = QUAD - shortage
    firsts = [index * wide - max(0, index - lacking) for index in range(QUAD)]
    skips = [(first - min(first, tiles - wide)) * 128 for first in firsts]
    lengths = [(wide - (index >= lacking)) * 128 for index in range(QUAD)]

    def attention_piece(index):
        cut = lambda w: lax.dynamic_slice_in_dim(w, index * att_width, att_width, 1)
        return jnp.concatenate(
            [cut(joined_master[c]) for c in range(3)] + [cut(outward_master)], axis=1
        ).astype(LOW)

    def hidden_cut(w, index):
        first = index * wide - jnp.maximum(0, index - lacking)
        start = jnp.minimum(first, tiles - wide)
        skip = (first - start) * 128
        length = jnp.where(index >= lacking, wide - 1, wide) * 128
        column = lax.broadcasted_iota(jnp.int32, (1, ff_width), 1)
        keep = (column >= skip) & (column < skip + length)
        part = lax.dynamic_slice_in_dim(w, start * 128, ff_width, 1)
        return jnp.where(keep, part, 0.0).astype(LOW)

    def gated_piece(index):
        return jnp.concatenate([hidden_cut(gated_master[c], index) for c in range(2)], axis=1)

    def downward_piece(index):
        return hidden_cut(downward_master, index)

    def other(bit):
        return jnp.bitwise_xor(place, bit)

    def pieces(make):
        return [make(other(bits)) for bits in range(QUAD)]

    def ordered(blocks):
        stacked = jnp.stack(blocks)
        return jnp.stack(
            [lax.dynamic_index_in_dim(stacked, other(j), 0, False) for j in range(QUAD)]
        )

    vectors_low = gather_small(vectors_master.astype(LOW))
    vectors_full = vectors_low.astype(F32)
    row_gain, row_shift = vectors_full[0:1], vectors_full[1:2]
    bias_at = (tp_index * QUAD + place) * att_width
    bias_here = lax.dynamic_slice_in_dim(vectors_full[2:5], bias_at, att_width, 1).reshape(1, 3 * att_width)

    own_rows, own_back = inputs[:, 0], cotangent[:, 0]
    line = ("a", "tp")
    rows_all = lax.all_gather(own_rows, line, axis=0).reshape(-1, depth)
    back_all = lax.all_gather(own_back, line, axis=0).reshape(-1, depth)

    def flat(weight):
        return weight.reshape(depth, weight.shape[-1])

    joined = exchange(pieces(attention_piece), (vectors_low,))
    joined_near = plane.gather_first(ordered(joined), joined[1:])
    gated = exchange(pieces(gated_piece), joined[1:])
    stage = [*joined_near[1:], *gated[1:], rows_all]
    gated_near = plane.gather_first(ordered(gated), stage)
    normed, xhat_all = norm_rows(rows_all, row_gain, row_shift)
    stage = [*gated_near[1:], normed]
    gated_weight, last = plane.gather_second(gated_near, stage)
    gated_weight = flat(gated_weight)
    downward = exchange(pieces(downward_piece), last)
    attention_weight, joined_last = plane.gather_second(joined_near, last)
    attention_weight = flat(attention_weight)
    downward_near = plane.gather_first(ordered(downward), [*downward[1:], *joined_last])
    downward_weight, last = plane.gather_second(downward_near, downward_near[1:])
    downward_weight = flat(downward_weight)
    activated, silu, slope = gate_up(normed, gated_weight)
    joined_out = times(
        normed, attention_weight, 0, 3 * att_width, F32, (activated, *downward[1:])
    )
    mixed_grad = times(back_all, attention_weight, 3, att_width, LOW, (joined_out,))
    mixed, joined_grad, bias_grad = attention(joined_out, mixed_grad, bias_here, downward_near[1:])

    def fold(term):
        return term.reshape(QUAD, depth // QUAD, term.shape[1])

    def homeward(total, gate):
        total = total.astype(LOW)
        return exchange(
            [lax.dynamic_index_in_dim(total, other(bits), 0, False) for bits in range(QUAD)], gate
        )

    def scatter_rows(part):
        folded = part.reshape(2 * QUAD, MICRO, 128, depth)
        return lax.psum_scatter(folded, line, scatter_dimension=0)

    out_part, _ = product_sum([(mixed, attention_weight, 3), (activated, downward_weight, 0)], depth)
    branch = scatter_rows(out_part)
    attention_term = weight_term([(joined_grad, normed), (mixed, back_all)], (out_part,))
    joined_known = plane.sum_first(fold(attention_term), ())
    gated_grad = gate_up_back(back_all, downward_weight, silu, slope, (attention_term,))
    gated_term = weight_term([(gated_grad, normed)], joined_known[1:])
    joined_total, last = plane.sum_second(joined_known, joined_known[1:])
    downward_term = weight_term([(activated, back_all)], (gated_term, *last))
    gated_known = plane.sum_first(fold(gated_term), last)
    joined_home = homeward(joined_total, last)
    grad_pairs = [(joined_grad, attention_weight, 0), (gated_grad, gated_weight, 0)]
    half_done, sums_low = product_sum(
        grad_pairs, depth, xhat_all, (downward_term, *gated_known[1:]), 0
    )
    gated_total, last = plane.sum_second(gated_known, gated_known[1:])
    downward_known = plane.sum_first(fold(downward_term), gated_known[1:])
    normed_grad_part, sums_high = product_sum(
        grad_pairs, depth, xhat_all, joined_home[1:], 1, half_done
    )
    stage = [*last, *downward_known[1:], *joined_home[1:], normed_grad_part]
    gated_home = homeward(gated_total, stage)
    downward_total, last = plane.sum_second(downward_known, stage)
    stage = [*gated_home[1:], *last]
    own_grad = scatter_rows(after(normed_grad_part, branch, *stage)).astype(F32)
    downward_home = homeward(downward_total, stage)
    sums = sums_low + sums_high
    branch = branch.astype(F32)

    def settled(home):
        return [block.astype(F32) for block in ordered(home)]

    downward_own, attention_own, gated_own = settled(downward_home), settled(joined_home), settled(gated_home)

    own_float = own_rows.astype(F32)
    outputs = (own_float + branch).astype(LOW)[:, None]
    average = jnp.mean(own_float, axis=-1, keepdims=True)
    centred_own = own_float - average
    inverse_own = lax.rsqrt(jnp.mean(centred_own * centred_own, axis=-1, keepdims=True) + EPS_NORM)
    xhat = centred_own * inverse_own
    scaled = own_grad * row_gain
    rows_grad = inverse_own * (
        scaled
        - jnp.mean(scaled, axis=-1, keepdims=True)
        - xhat * jnp.mean(scaled * xhat, axis=-1, keepdims=True)
    )
    input_grad = (own_back.astype(F32) + rows_grad).astype(LOW)[:, None]

    bias_wide = lax.dynamic_update_slice(
        jnp.zeros((3, depth), F32), bias_grad.reshape(3, att_width), (0, bias_at)
    )
    sums = jnp.sum(sums.reshape(2, 8, depth), axis=1)
    squares = jnp.concatenate(
        [sum(jnp.sum(block * block, axis=0) for block in own) for own in (downward_own, attention_own, gated_own)]
    )
    rest = 3 * depth - squares.shape[0]
    everywhere = sum_small(
        jnp.concatenate([sums, bias_wide, jnp.pad(squares, (0, rest)).reshape(3, depth)], axis=0)
    )
    vectors_sum = everywhere[:5]
    vectors_grad = lax.dynamic_slice_in_dim(
        vectors_sum, (place * plane.count + plane.at) * rows_here, rows_here, 1
    )

    def attention_columns(c):
        cut = slice(c * att_width, (c + 1) * att_width)
        return jnp.concatenate([piece[:, cut] for piece in attention_own], axis=1)

    joined_grads = jnp.stack([attention_columns(c) for c in range(3)])
    outward_grads = attention_columns(3)

    def hidden_columns(pieces, c):
        return jnp.concatenate(
            [
                piece[:, c * ff_width + skip : c * ff_width + skip + length]
                for piece, skip, length in zip(pieces, skips, lengths)
            ],
            axis=1,
        )

    gated_grads = jnp.stack([hidden_columns(gated_own, c) for c in range(2)])
    downward_grads = hidden_columns(downward_own, 0)

    grad_norm = jnp.sqrt(jnp.sum(everywhere[5:]) + jnp.sum(vectors_sum * vectors_sum))
    factor = jnp.minimum(1.0, CLIP / (grad_norm + 1e-06))
    ff_total = ff_here * tp_count
    return (
        outputs,
        input_grad,
        grad_norm,
        *adamw(joined_master, joined_first, joined_second, joined_grads, factor, depth ** (-0.5), DECAY),
        *adamw(outward_master, outward_first, outward_second, outward_grads, factor, (depth // 32) ** (-0.5), DECAY),
        *adamw(gated_master, gated_first, gated_second, gated_grads, factor, depth ** (-0.5), DECAY),
        *adamw(downward_master, downward_first, downward_second, downward_grads, factor, ff_total ** (-0.5), DECAY),
        *adamw(vectors_master, vectors_first, vectors_second, vectors_grad, factor, SMALL_RATE, 0.0),
    )


def solution(mesh):
    fsdp, tp = mesh.shape["fsdp"], mesh.shape["tp"]
    fine = Mesh(mesh.devices.reshape(QUAD, 2, fsdp // QUAD // 2, tp), ("a", "y", "x", "tp"))
    every = ("a", "y", "x")
    rows = P(None, every, "tp", None)
    stacked = P(None, every, "tp")
    flat = P(every, "tp")
    vectors = P(None, every)
    return jax.shard_map(
        on_device,
        mesh=fine,
        in_specs=(rows,) * 2 + (stacked,) * 3 + (flat,) * 3 + (stacked,) * 3 + (flat,) * 3 + (vectors,) * 3,
        out_specs=(rows,) * 2
        + (P(),)
        + (stacked,) * 4
        + (flat,) * 4
        + (stacked,) * 4
        + (flat,) * 4
        + (vectors,) * 4,
        check_vma=False,
    )
```

```python
import functools
import jax
import jax.numpy as jnp
from jax import lax
from jax.experimental import pallas as pl
from jax.experimental.pallas import tpu as pltpu
from jax.sharding import Mesh
from jax.sharding import PartitionSpec as P

HD = 64
ROT = 16
MICRO = 2
STEP = 5
QUAD = 4

EPS_NORM = 1e-05
CLIP = 1.0
BETA_ONE = 0.5
BETA_TWO = 0.5
ADAM_EPS = 1e-08
DECAY = 0.1
SMALL_RATE = 0.2
ROPE_BASE = 10000.0
LOW = jnp.bfloat16
F32 = jnp.float32
SWAP = [(0, 1), (1, 0)]


def nn(left, right):
    return lax.dot_general(left, right, (((1,), (0,)), ((), ())), preferred_element_type=F32)


def nt(left, right):
    return lax.dot_general(left, right, (((1,), (1,)), ((), ())), preferred_element_type=F32)


def tn(left, right):
    return lax.dot_general(left, right, (((0,), (0,)), ((), ())), preferred_element_type=F32)


def swap(value, axis):
    return lax.ppermute(value, axis, SWAP)


ANYWHERE = pl.BlockSpec(memory_space=pl.ANY)
BIG = 56 * 1024 * 1024


def launch(kernel, name, grid, operands, in_specs, out_specs, out_shape, flops, deps=(), lead=(), aliases=None):
    count, extra, ahead = len(operands), len(deps), len(lead)

    def run(*refs):
        refs = refs[ahead:]
        kernel(*refs[:count], *refs[count + extra :])

    shapes = out_shape if isinstance(out_shape, list) else [out_shape]
    moved = sum(v.size * v.dtype.itemsize for v in operands)
    moved += sum(s.size * s.dtype.itemsize for s in shapes)
    return pl.pallas_call(
        run,
        grid_spec=pltpu.PrefetchScalarGridSpec(
            num_scalar_prefetch=ahead,
            grid=grid,
            in_specs=list(in_specs) + [ANYWHERE] * extra,
            out_specs=out_specs,
        ),
        out_shape=out_shape,
        input_output_aliases={len(lead) + k: v for k, v in (aliases or {}).items()},
        cost_estimate=pl.CostEstimate(flops=flops, bytes_accessed=moved, transcendentals=0),
        compiler_params=pltpu.CompilerParams(vmem_limit_bytes=BIG),
        name=name,
    )(*lead, *operands, *deps)


def gate_kernel(*refs):
    pass


def after(value, *others):
    if not others:
        return value
    return pl.pallas_call(
        gate_kernel,
        in_specs=[ANYWHERE] * (1 + len(others)),
        out_specs=ANYWHERE,
        out_shape=jax.ShapeDtypeStruct(value.shape, value.dtype),
        input_output_aliases={0: 0},
        name="after",
    )(value, *others)


def blank(shape, dtype):
    return pl.pallas_call(
        gate_kernel,
        out_specs=ANYWHERE,
        out_shape=jax.ShapeDtypeStruct(shape, dtype),
        name="blank",
    )()


def held(values, gate):
    return [after(value, *gate) for value in values]


def exchange(blocks, gate):
    out = held(blocks[1:], gate)
    return [blocks[0]] + [
        lax.ppermute(block, "a", [(i, i ^ bit) for i in range(QUAD)])
        for bit, block in enumerate(out, 1)
    ]


class Plane:
    def __init__(self):
        self.square = lax.axis_size("x") == 2
        self.count = lax.axis_size("x") * lax.axis_size("y")
        self.at = lax.axis_index(("y", "x"))

    def gather_first(self, mine, gate):
        if not self.square:
            return (mine,)
        to_x, to_y = held([mine, mine], gate)
        return (mine, swap(to_x, "x"), swap(to_y, "y"))

    def gather_second(self, known, gate):
        mine = known[0]
        if not self.square:
            return lax.all_gather(mine, ("y", "x"), axis=1, tiled=True), ()
        half = QUAD // 2
        upper, lower = held([known[1][:half], known[2][half:]], gate)
        last = (swap(upper, "y"), swap(lower, "x"))
        rows = mine.shape[1]
        whole = blank((QUAD, self.count * rows, mine.shape[2]), mine.dtype)
        for bits, block, first in (
            (0, mine, 0),
            (1, known[1], 0),
            (2, known[2], 0),
            (3, last[0], 0),
            (3, last[1], half),
        ):
            at = jnp.bitwise_xor(self.at, bits) * rows
            whole = lax.dynamic_update_slice(whole, block, (first, at, 0))
        return whole, last

    def part(self, term, bits):
        rows = term.shape[1] // self.count
        return lax.dynamic_slice_in_dim(term, jnp.bitwise_xor(self.at, bits) * rows, rows, 1)

    def sum_first(self, term, gate):
        if not self.square:
            return (term,)
        half = QUAD // 2
        across = self.part(term, 3)
        upper, lower = held([across[:half], across[half:]], gate)
        return (term, swap(upper, "y"), swap(lower, "x"))

    def sum_second(self, known, gate):
        term = known[0]
        if not self.square:
            return lax.psum_scatter(term, ("y", "x"), scatter_dimension=1, tiled=True), ()
        half = QUAD // 2
        to_x, to_y = self.part(term, 1), self.part(term, 2)
        to_x = jnp.concatenate([add_low(to_x[:half], known[1]), to_x[half:]])
        to_y = jnp.concatenate([to_y[:half], add_low(to_y[half:], known[2])])
        to_x, to_y = held([to_x, to_y], gate)
        last = (swap(to_x, "x"), swap(to_y, "y"))
        total = self.part(term, 0).astype(F32) + last[0].astype(F32) + last[1].astype(F32)
        return total, last


def add_low(left, right):
    return (left.astype(F32) + right.astype(F32)).astype(LOW)


def bits(axis):
    found, bit = [], 1
    count, at = lax.axis_size(axis), lax.axis_index(axis)
    while bit < count:
        found.append((axis, [(i, i ^ bit) for i in range(count)], (at // bit) % 2))
        bit *= 2
    return found


def gather_small(value):
    for axis, pairs, bit in bits("x") + bits("y") + bits("a"):
        other = lax.ppermute(value, axis, pairs)
        value = jnp.where(
            bit == 0,
            jnp.concatenate([value, other], axis=-1),
            jnp.concatenate([other, value], axis=-1),
        )
    return value


def sum_small(value):
    for axis, pairs, bit in bits("tp") + bits("x") + bits("y") + bits("a"):
        value = value + lax.ppermute(value, axis, pairs)
    return value


def attention_kernel(
    mask_ref, cos_ref, left_ref, right_ref, bias_ref, joined_ref, back_ref, mixed_ref, grad_ref, bias_grad_ref
):
    rows, width = cos_ref.shape
    heads = width // HD
    scale = HD ** (-0.5)
    joined = joined_ref[...].reshape(rows, 3 * width) + bias_ref[0:1, :]
    cos, left, right = cos_ref[...], left_ref[...], right_ref[...]

    def turn(v):
        return v * cos + pltpu.roll(v, width - ROT // 2, 1) * left + pltpu.roll(v, ROT // 2, 1) * right

    def turn_back(g):
        return g * cos - (pltpu.roll(g, width - ROT // 2, 1) * left + pltpu.roll(g, ROT // 2, 1) * right)

    query = turn(joined[:, :width]).astype(LOW)
    keys = turn(joined[:, width : 2 * width]).astype(LOW)
    values = joined[:, 2 * width :].astype(LOW)
    back = back_ref[...].reshape(rows, width)
    mask = mask_ref[...]
    mixed, d_query, d_keys, d_values = [], [], [], []
    for head in range(heads):
        cut = slice(head * HD, (head + 1) * HD)
        q, k, v, g = query[:, cut], keys[:, cut], values[:, cut], back[:, cut]
        q = q * jnp.asarray(scale, LOW)
        scores = nt(q, k) + mask
        peak = jnp.max(scores, axis=-1, keepdims=True)
        raised = jnp.exp(scores - peak)
        full = raised * (1.0 / jnp.sum(raised, axis=-1, keepdims=True))
        probs = full.astype(LOW)
        mixed.append(nn(probs, v))
        prob_grad = nt(g, v)
        weighted = full * prob_grad
        inner = jnp.sum(weighted, axis=-1, keepdims=True)
        score_grad = (weighted - full * inner).astype(LOW)
        d_query.append(nn(score_grad, k) * scale)
        d_keys.append(tn(score_grad, q))
        d_values.append(tn(probs, g))
    mixed_ref[...] = jnp.concatenate(mixed, axis=-1).astype(LOW).reshape(mixed_ref.shape)
    out = jnp.concatenate(
        [
            turn_back(jnp.concatenate(d_query, axis=-1)),
            turn_back(jnp.concatenate(d_keys, axis=-1)),
            jnp.concatenate(d_values, axis=-1),
        ],
        axis=-1,
    ).astype(LOW)
    grad_ref[...] = out.reshape(grad_ref.shape)

    @pl.when(pl.program_id(0) == 0)
    def _():
        bias_grad_ref[...] = jnp.zeros_like(bias_grad_ref)

    sums = jnp.sum(out.astype(F32).reshape(rows // 8, 8, 3 * width), axis=0)
    bias_grad_ref[...] += sums


def attention(joined, back, bias, deps=()):
    tokens, width = back.shape
    half = 128
    seqs = tokens // (2 * half)
    length = 2 * half
    position = jnp.arange(length)
    mask = jnp.where(position[:, None] >= position[None, :], 0.0, -jnp.inf).astype(F32)
    frequency = ROPE_BASE ** (-(2.0 * jnp.arange(ROT // 2, dtype=F32)) / ROT)
    angles = position.astype(F32)[:, None] * frequency[None, :]
    cosine, sine = jnp.cos(angles), jnp.sin(angles)
    rest = jnp.ones((length, HD - ROT), F32)
    nothing = jnp.zeros((length, ROT // 2), F32)
    heads = width // HD
    cos = jnp.tile(jnp.concatenate([cosine, cosine, rest], 1), (1, heads))
    left = jnp.tile(jnp.concatenate([-sine, nothing, 0.0 * rest], 1), (1, heads))
    right = jnp.tile(jnp.concatenate([nothing, sine, 0.0 * rest], 1), (1, heads))
    rows = lambda i: (i // MICRO, 0, i % MICRO, 0, 0)
    shape = lambda w: (seqs // MICRO, 2, MICRO, half, w)
    mixed, grad, bias_grad = launch(
        attention_kernel,
        "attention_both_ways",
        (seqs,),
        [mask, cos, left, right, bias, joined.reshape(shape(3 * width)), back.reshape(shape(width))],
        [
            pl.BlockSpec((length, length), fixed),
            pl.BlockSpec((length, width), fixed),
            pl.BlockSpec((length, width), fixed),
            pl.BlockSpec((length, width), fixed),
            pl.BlockSpec((1, 3 * width), fixed),
            pl.BlockSpec((1, 2, 1, half, 3 * width), rows),
            pl.BlockSpec((1, 2, 1, half, width), rows),
        ],
        [
            pl.BlockSpec((1, 2, 1, half, width), rows),
            pl.BlockSpec((1, 2, 1, half, 3 * width), rows),
            pl.BlockSpec((8, 3 * width), fixed),
        ],
        [
            jax.ShapeDtypeStruct(shape(width), LOW),
            jax.ShapeDtypeStruct(shape(3 * width), LOW),
            jax.ShapeDtypeStruct((8, 3 * width), F32),
        ],
        seqs * heads * 7 * 2 * length * length * HD * 4,
        deps,
    )
    return (
        mixed.reshape(tokens, width),
        grad.reshape(tokens, 3 * width),
        jnp.sum(bias_grad, axis=0),
    )


def norm_kernel(gain_ref, shift_ref, rows_ref, normed_ref, xhat_ref):
    rows = rows_ref[...].astype(F32)
    average = jnp.mean(rows, axis=-1, keepdims=True)
    centred = rows - average
    variance = jnp.mean(centred * centred, axis=-1, keepdims=True)
    xhat = centred * lax.rsqrt(variance + EPS_NORM)
    xhat_ref[...] = xhat.astype(LOW)
    normed_ref[...] = (xhat * gain_ref[...] + shift_ref[...]).astype(LOW)


def by_row(i):
    return (i, 0)


def fixed(*grid):
    return (0, 0)


def norm_rows(rows, gain, shift, deps=()):
    tokens, depth = rows.shape
    tall = 256
    return launch(
        norm_kernel,
        "norm_rows",
        (tokens // tall,),
        [gain, shift, rows],
        [pl.BlockSpec((1, depth), fixed)] * 2 + [pl.BlockSpec((tall, depth), by_row)],
        [pl.BlockSpec((tall, depth), by_row)] * 2,
        [jax.ShapeDtypeStruct((tokens, depth), LOW)] * 2,
        20 * tokens * depth,
        deps,
    )


def columns_of(weight, at, width):
    return pl.BlockSpec((weight.shape[0], width), lambda i: (0, at))


def times_kernel(rows_ref, weight_ref, out_ref):
    out_ref[...] = nn(rows_ref[...], weight_ref[...]).astype(out_ref.dtype)


def times(rows, weight, at, width, dtype, deps=()):
    tokens, depth = rows.shape
    tall = 512
    return launch(
        times_kernel,
        "times",
        (tokens // tall,),
        [rows, weight],
        [pl.BlockSpec((tall, depth), by_row), columns_of(weight, at, width)],
        pl.BlockSpec((tall, width), by_row),
        jax.ShapeDtypeStruct((tokens, width), dtype),
        2 * tokens * depth * width,
        deps,
    )


def gate_up_kernel(rows_ref, weight_ref, act_ref, silu_ref, slope_ref):
    width = silu_ref.shape[1]
    both = nn(rows_ref[...], weight_ref[...])
    gate, up = both[:, :width], both[:, width:]
    sigma = 1.0 / (1.0 + jnp.exp(-gate))
    silu = gate * sigma
    act_ref[...] = (silu * up).astype(LOW)
    silu_ref[...] = silu
    slope_ref[...] = up * sigma * (1.0 + gate * (1.0 - sigma))


def gate_up(rows, weight, deps=()):
    tokens, depth = rows.shape
    width = weight.shape[1] // 2
    tall = 512
    return launch(
        gate_up_kernel,
        "gate_up",
        (tokens // tall,),
        [rows, weight],
        [pl.BlockSpec((tall, depth), by_row), pl.BlockSpec(weight.shape, fixed)],
        [pl.BlockSpec((tall, width), by_row)] * 3,
        [jax.ShapeDtypeStruct((tokens, width), dtype) for dtype in (LOW, F32, F32)],
        4 * tokens * depth * width,
        deps,
    )


def gate_up_back_kernel(rows_ref, weight_ref, silu_ref, slope_ref, out_ref):
    width = silu_ref.shape[1]
    act_grad = nn(rows_ref[...], weight_ref[...])
    out_ref[:, :width] = (act_grad * slope_ref[...]).astype(LOW)
    out_ref[:, width:] = (act_grad * silu_ref[...]).astype(LOW)


def gate_up_back(rows, weight, silu, slope, deps=()):
    tokens, depth = rows.shape
    width = weight.shape[1]
    tall = 512
    return launch(
        gate_up_back_kernel,
        "gate_up_back",
        (tokens // tall,),
        [rows, weight, silu, slope],
        [pl.BlockSpec((tall, depth), by_row), pl.BlockSpec(weight.shape, fixed)]
        + [pl.BlockSpec((tall, width), by_row)] * 2,
        pl.BlockSpec((tall, 2 * width), by_row),
        jax.ShapeDtypeStruct((tokens, 2 * width), LOW),
        2 * tokens * depth * width,
        deps,
    )


def term_kernel(*refs):
    out_ref = refs[-1]
    at = 0
    for grads_ref, rows_ref in zip(refs[0:-1:2], refs[1:-1:2]):
        width = grads_ref.shape[1]
        out_ref[:, at : at + width] = tn(rows_ref[...], grads_ref[...]).astype(LOW)
        at += width


def weight_term(items, deps=()):
    operands, in_specs = [], []
    broad = 512
    for grads, rows in items:
        operands += [grads, rows]
        in_specs.append(pl.BlockSpec(grads.shape, fixed))
        in_specs.append(pl.BlockSpec((rows.shape[0], broad), lambda j: (0, j)))
    tokens, depth = rows.shape
    width = sum(grads.shape[1] for grads, _ in items)
    return launch(
        term_kernel,
        "weight_term",
        (depth // broad,),
        operands,
        in_specs,
        pl.BlockSpec((broad, width), by_row),
        jax.ShapeDtypeStruct((depth, width), LOW),
        2 * tokens * depth * width,
        deps,
    )


def product_kernel(terms, with_xhat, *refs):
    lefts, rights, rest = refs[:terms], refs[terms : 2 * terms], refs[2 * terms :]
    total = nt(lefts[0][...], rights[0][...])
    for left, right in zip(lefts[1:], rights[1:]):
        total += nt(left[...], right[...])
    if not with_xhat:
        rest[-1][...] = total.astype(LOW)
        return
    xhat_ref, out_ref, sums_ref = rest[0], rest[-2], rest[-1]
    out_ref[...] = total.astype(LOW)
    xhat = xhat_ref[...].astype(F32)

    @pl.when(pl.program_id(0) == 0)
    def _():
        sums_ref[...] = jnp.zeros_like(sums_ref)

    tall = total.shape[0] // 8
    sums_ref[0:8, :] += jnp.sum((total * xhat).reshape(tall, 8, -1), axis=0)
    sums_ref[8:16, :] += jnp.sum(total.reshape(tall, 8, -1), axis=0)


def product_sum(pairs, depth, xhat=None, deps=(), part=None, into=None):
    tall = 512
    terms = len(pairs)
    rows = pairs[0][0].shape[0]
    steps = rows // tall if part is None else rows // tall // 2
    first = steps * (part or 0)
    below = lambda i: (i + first, 0)
    in_specs = [pl.BlockSpec((tall, left.shape[1]), below) for left, _, _ in pairs]
    in_specs += [columns_of(right, at, left.shape[1]) for left, right, at in pairs]
    operands = [p[0] for p in pairs] + [p[1] for p in pairs]
    out_specs = [pl.BlockSpec((tall, depth), below)]
    out_shape = [jax.ShapeDtypeStruct((rows, depth), LOW)]
    if xhat is not None:
        in_specs.append(pl.BlockSpec((tall, depth), below))
        operands.append(xhat)
        out_specs.append(pl.BlockSpec((16, depth), fixed))
        out_shape.append(jax.ShapeDtypeStruct((16, depth), F32))
    aliases = {}
    if into is not None:
        aliases = {len(operands): 0}
        in_specs.append(ANYWHERE)
        operands.append(into)
    deep = sum(left.shape[1] for left, _, _ in pairs)
    found = launch(
        functools.partial(product_kernel, terms, xhat is not None),
        "product_sum",
        (steps,),
        operands,
        in_specs,
        out_specs,
        out_shape,
        2 * steps * tall * depth * deep,
        deps,
        (),
        aliases,
    )
    return found if xhat is not None else (found[0], None)


def adamw(master, first_old, second_old, gradient, factor, step_rate, weight_decay):
    clipped = gradient * factor
    moment = BETA_ONE * first_old + (1.0 - BETA_ONE) * clipped
    variance = BETA_TWO * second_old + (1.0 - BETA_TWO) * clipped * clipped
    moment_hat = moment / (1.0 - BETA_ONE**STEP)
    variance_hat = variance / (1.0 - BETA_TWO**STEP)
    updated = master - step_rate * (
        moment_hat / (jnp.sqrt(variance_hat) + ADAM_EPS) + weight_decay * master
    )
    return (updated, moment, variance, updated.astype(LOW))


def on_device(
    inputs,
    cotangent,
    joined_master,
    joined_first,
    joined_second,
    outward_master,
    outward_first,
    outward_second,
    gated_master,
    gated_first,
    gated_second,
    downward_master,
    downward_first,
    downward_second,
    vectors_master,
    vectors_first,
    vectors_second,
):
    tp_count = lax.axis_size("tp")
    plane = Plane()
    place = lax.axis_index("a")
    tp_index = lax.axis_index("tp")
    depth = inputs.shape[-1]
    rows_here = joined_master.shape[1]
    att_width = joined_master.shape[2] // QUAD
    ff_here = gated_master.shape[2]
    tiles = ff_here // 128
    wide = -(-tiles // QUAD)
    ff_width = wide * 128
    shortage = wide * QUAD - tiles

    lacking = QUAD - shortage
    firsts = [index * wide - max(0, index - lacking) for index in range(QUAD)]
    skips = [(first - min(first, tiles - wide)) * 128 for first in firsts]
    lengths = [(wide - (index >= lacking)) * 128 for index in range(QUAD)]

    def attention_piece(index):
        cut = lambda w: lax.dynamic_slice_in_dim(w, index * att_width, att_width, 1)
        return jnp.concatenate(
            [cut(joined_master[c]) for c in range(3)] + [cut(outward_master)], axis=1
        ).astype(LOW)

    def hidden_cut(w, index):
        first = index * wide - jnp.maximum(0, index - lacking)
        start = jnp.minimum(first, tiles - wide)
        skip = (first - start) * 128
        length = jnp.where(index >= lacking, wide - 1, wide) * 128
        column = lax.broadcasted_iota(jnp.int32, (1, ff_width), 1)
        keep = (column >= skip) & (column < skip + length)
        part = lax.dynamic_slice_in_dim(w, start * 128, ff_width, 1)
        return jnp.where(keep, part, 0.0).astype(LOW)

    def gated_piece(index):
        return jnp.concatenate([hidden_cut(gated_master[c], index) for c in range(2)], axis=1)

    def downward_piece(index):
        return hidden_cut(downward_master, index)

    def other(bit):
        return jnp.bitwise_xor(place, bit)

    def pieces(make):
        return [make(other(bits)) for bits in range(QUAD)]

    def ordered(blocks):
        stacked = jnp.stack(blocks)
        return jnp.stack(
            [lax.dynamic_index_in_dim(stacked, other(j), 0, False) for j in range(QUAD)]
        )

    vectors_low = gather_small(vectors_master.astype(LOW))
    vectors_full = vectors_low.astype(F32)
    row_gain, row_shift = vectors_full[0:1], vectors_full[1:2]
    bias_at = (tp_index * QUAD + place) * att_width
    bias_here = lax.dynamic_slice_in_dim(vectors_full[2:5], bias_at, att_width, 1).reshape(1, 3 * att_width)

    own_rows, own_back = inputs[:, 0], cotangent[:, 0]
    line = ("a", "tp")
    rows_all = lax.all_gather(own_rows, line, axis=0).reshape(-1, depth)
    back_all = lax.all_gather(own_back, line, axis=0).reshape(-1, depth)

    def flat(weight):
        return weight.reshape(depth, weight.shape[-1])

    joined = exchange(pieces(attention_piece), (vectors_low,))
    joined_near = plane.gather_first(ordered(joined), joined[1:])
    gated = exchange(pieces(gated_piece), joined[1:])
    stage = [*joined_near[1:], *gated[1:], rows_all]
    gated_near = plane.gather_first(ordered(gated), stage)
    attention_weight, joined_last = plane.gather_second(joined_near, stage)
    attention_weight = flat(attention_weight)
    normed, xhat_all = norm_rows(rows_all, row_gain, row_shift)
    downward = exchange(pieces(downward_piece), (normed,))
    stage = [*gated_near[1:], *joined_last, normed]
    gated_weight, last = plane.gather_second(gated_near, stage)
    gated_weight = flat(gated_weight)
    joined_out = times(normed, attention_weight, 0, 3 * att_width, F32, downward[1:])
    activated, silu, slope = gate_up(normed, gated_weight, (joined_out,))
    downward_near = plane.gather_first(ordered(downward), [*downward[1:], *last])
    downward_weight, last = plane.gather_second(downward_near, downward_near[1:])
    downward_weight = flat(downward_weight)
    mixed_grad = times(back_all, attention_weight, 3, att_width, LOW, (activated,))
    mixed, joined_grad, bias_grad = attention(joined_out, mixed_grad, bias_here, downward_near[1:])

    def fold(term):
        return term.reshape(QUAD, depth // QUAD, term.shape[1])

    def homeward(total, gate):
        total = total.astype(LOW)
        return exchange(
            [lax.dynamic_index_in_dim(total, other(bits), 0, False) for bits in range(QUAD)], gate
        )

    def scatter_rows(part):
        folded = part.reshape(2 * QUAD, MICRO, 128, depth)
        return lax.psum_scatter(folded, line, scatter_dimension=0)

    out_part, _ = product_sum([(mixed, attention_weight, 3), (activated, downward_weight, 0)], depth)
    branch = scatter_rows(out_part)
    attention_term = weight_term([(joined_grad, normed), (mixed, back_all)], (out_part,))
    joined_known = plane.sum_first(fold(attention_term), ())
    gated_grad = gate_up_back(back_all, downward_weight, silu, slope, (attention_term,))
    gated_term = weight_term([(gated_grad, normed)], joined_known[1:])
    joined_total, last = plane.sum_second(joined_known, joined_known[1:])
    downward_term = weight_term([(activated, back_all)], (gated_term, *last))
    gated_known = plane.sum_first(fold(gated_term), last)
    joined_home = homeward(joined_total, last)
    grad_pairs = [(joined_grad, attention_weight, 0), (gated_grad, gated_weight, 0)]
    half_done, sums_low = product_sum(
        grad_pairs, depth, xhat_all, (downward_term, *gated_known[1:]), 0
    )
    gated_total, last = plane.sum_second(gated_known, gated_known[1:])
    downward_known = plane.sum_first(fold(downward_term), gated_known[1:])
    normed_grad_part, sums_high = product_sum(
        grad_pairs, depth, xhat_all, joined_home[1:], 1, half_done
    )
    stage = [*last, *downward_known[1:], *joined_home[1:], normed_grad_part]
    gated_home = homeward(gated_total, stage)
    downward_total, last = plane.sum_second(downward_known, stage)
    stage = [*gated_home[1:], *last]
    own_grad = scatter_rows(after(normed_grad_part, branch, *stage)).astype(F32)
    downward_home = homeward(downward_total, last)
    sums = sums_low + sums_high
    branch = branch.astype(F32)

    def settled(home):
        return [block.astype(F32) for block in ordered(home)]

    downward_own, attention_own, gated_own = settled(downward_home), settled(joined_home), settled(gated_home)

    own_float = own_rows.astype(F32)
    outputs = (own_float + branch).astype(LOW)[:, None]
    average = jnp.mean(own_float, axis=-1, keepdims=True)
    centred_own = own_float - average
    inverse_own = lax.rsqrt(jnp.mean(centred_own * centred_own, axis=-1, keepdims=True) + EPS_NORM)
    xhat = centred_own * inverse_own
    scaled = own_grad * row_gain
    rows_grad = inverse_own * (
        scaled
        - jnp.mean(scaled, axis=-1, keepdims=True)
        - xhat * jnp.mean(scaled * xhat, axis=-1, keepdims=True)
    )
    input_grad = (own_back.astype(F32) + rows_grad).astype(LOW)[:, None]

    bias_wide = lax.dynamic_update_slice(
        jnp.zeros((3, depth), F32), bias_grad.reshape(3, att_width), (0, bias_at)
    )
    sums = jnp.sum(sums.reshape(2, 8, depth), axis=1)
    squares = jnp.concatenate(
        [sum(jnp.sum(block * block, axis=0) for block in own) for own in (downward_own, attention_own, gated_own)]
    )
    rest = 3 * depth - squares.shape[0]
    everywhere = sum_small(
        jnp.concatenate([sums, bias_wide, jnp.pad(squares, (0, rest)).reshape(3, depth)], axis=0)
    )
    vectors_sum = everywhere[:5]
    vectors_grad = lax.dynamic_slice_in_dim(
        vectors_sum, (place * plane.count + plane.at) * rows_here, rows_here, 1
    )

    def attention_columns(c):
        cut = slice(c * att_width, (c + 1) * att_width)
        return jnp.concatenate([piece[:, cut] for piece in attention_own], axis=1)

    joined_grads = jnp.stack([attention_columns(c) for c in range(3)])
    outward_grads = attention_columns(3)

    def hidden_columns(pieces, c):
        return jnp.concatenate(
            [
                piece[:, c * ff_width + skip : c * ff_width + skip + length]
                for piece, skip, length in zip(pieces, skips, lengths)
            ],
            axis=1,
        )

    gated_grads = jnp.stack([hidden_columns(gated_own, c) for c in range(2)])
    downward_grads = hidden_columns(downward_own, 0)

    grad_norm = jnp.sqrt(jnp.sum(everywhere[5:]) + jnp.sum(vectors_sum * vectors_sum))
    factor = jnp.minimum(1.0, CLIP / (grad_norm + 1e-06))
    ff_total = ff_here * tp_count
    return (
        outputs,
        input_grad,
        grad_norm,
        *adamw(joined_master, joined_first, joined_second, joined_grads, factor, depth ** (-0.5), DECAY),
        *adamw(outward_master, outward_first, outward_second, outward_grads, factor, (depth // 32) ** (-0.5), DECAY),
        *adamw(gated_master, gated_first, gated_second, gated_grads, factor, depth ** (-0.5), DECAY),
        *adamw(downward_master, downward_first, downward_second, downward_grads, factor, ff_total ** (-0.5), DECAY),
        *adamw(vectors_master, vectors_first, vectors_second, vectors_grad, factor, SMALL_RATE, 0.0),
    )


def solution(mesh):
    fsdp, tp = mesh.shape["fsdp"], mesh.shape["tp"]
    fine = Mesh(mesh.devices.reshape(QUAD, 2, fsdp // QUAD // 2, tp), ("a", "y", "x", "tp"))
    every = ("a", "y", "x")
    rows = P(None, every, "tp", None)
    stacked = P(None, every, "tp")
    flat = P(every, "tp")
    vectors = P(None, every)
    return jax.shard_map(
        on_device,
        mesh=fine,
        in_specs=(rows,) * 2 + (stacked,) * 3 + (flat,) * 3 + (stacked,) * 3 + (flat,) * 3 + (vectors,) * 3,
        out_specs=(rows,) * 2
        + (P(),)
        + (stacked,) * 4
        + (flat,) * 4
        + (stacked,) * 4
        + (flat,) * 4
        + (vectors,) * 4,
        check_vma=False,
    )
```
